32 devices in a mesh: fc: 8 (over z, core), tok: 4 (over y, x).
Axes of the slice: x: 2, y: 2, z: 4, core: 2. Of those that a mesh axis runs over, the one named last changes fastest.
Arguments:
- tokens: bfloat16 [8, 32, 128, 1024], P('fc', 'tok'), may hold values from -6 to 6
- slot_keys: bfloat16 [1024, 256], replicated, may hold values from -2 to 2
- norm_gain: float32 [1024], replicated, may hold values from 0.25 to 1.75
- slot_gain: float32 [1024], replicated, may hold values from 0.25 to 1.75
- w_in: bfloat16 [64, 1024, 512], P(('fc', 'tok')), may hold values from -0.1875 to 0.1875
- w_out: bfloat16 [64, 512, 1024], P(('fc', 'tok')), may hold values from -0.25 to 0.25
- conv_weight: float32 [7, 7, 1024], replicated, may hold values from -0.875 to 0.875
- ln_gain: float32 [1024], replicated, may hold values from 0.25 to 1.75
- proj: bfloat16 [1024, 1024], replicated, may hold values from -0.1875 to 0.1875
- layer_scale: float32 [1024], replicated, may hold values from 0.25 to 1.75
Outputs:
- fields: bfloat16 [8, 32, 128, 1024], P('fc', 'tok')
The draws below stay inside these ranges and needn't reach their ends.
All inputs are finite; a program needn't handle non-finite values.
Results may differ from the reference program's by a relative error of at most 0.008.
The reference program's roundings to bfloat16 on the way (of `normed`, `dispatch`, `slot_in`, `hidden`, `slot_out`, `combine`, `state` and `normal`) count: a program that leaves them out, or rounds other values in their place, can miss the bound.
Values may be sent and summed in bfloat16 or wider, within the bound.
No kernel may reach another device: no remote copies, remote signals or barrier semaphores. Data moves between devices by JAX's collectives and lax.ppermute only.
A program may use at most 64 MiB of HBM per device.

```python
import jax
import jax.numpy as jnp
from jax import lax

D = 1024
FF = 512
SLOTS_EXP = 4
KSIZE = 7
COLS = 128
MEMBERS = 8
ROWS = 32
EXPERTS = 64
SLOTS = 256


def draw_slot_keys(key, part):
    base = jax.random.truncated_normal(jax.random.fold_in(key, 1), -6.0, 6.0, (D, SLOTS), jnp.float32) * D ** (-0.5)
    return base.astype(jnp.bfloat16)


def draw_tokens(key, part):
    base = jax.random.truncated_normal(jax.random.fold_in(key, 5), -6.0, 6.0, (MEMBERS, ROWS, COLS, D), jnp.float32)
    return base.astype(jnp.bfloat16)


def block_levels(key, extent, cuts, smallest, largest):
    def one(axis_at, blocks):
        steps = jax.random.uniform(jax.random.fold_in(jax.random.fold_in(key, 6), axis_at), (blocks,), jnp.float32, smallest / len(cuts), largest / len(cuts))
        return jnp.repeat(jnp.exp(steps), extent[axis_at] // blocks).reshape((-1,) + (1,) * (len(extent) - axis_at - 1))

    level = one(*cuts[0])
    for cut in cuts[1:]:
        level = level * one(*cut)
    return level


def gaussian(rng, dims, scale, reach, cuts=(), dtype=jnp.bfloat16):
    level = block_levels(rng, dims, cuts, -0.22, 0.18) if cuts else 1.0
    drawn = jax.random.normal(rng, dims, jnp.float32) * scale * level
    return jnp.minimum(jnp.maximum(drawn, -reach), reach).astype(dtype)


def setup_inputs(seed: int = 0) -> dict:
    keys = jax.random.split(jax.random.key(seed), 11)
    tokens = draw_tokens(jax.random.fold_in(keys[10], 71), 0)
    slot_keys = draw_slot_keys(jax.random.fold_in(keys[10], 71), 0)
    norm_gain = jnp.clip(1.0 + 0.15 * jax.random.normal(keys[2], (D,), jnp.float32), 0.25, 1.75)
    slot_gain = jnp.clip(1.0 + 0.15 * jax.random.normal(keys[3], (D,), jnp.float32), 0.25, 1.75)
    w_in = gaussian(keys[4], (EXPERTS, D, FF), D ** -0.5, 0.1875, ((0, 32),))
    w_out = gaussian(keys[5], (EXPERTS, FF, D), FF ** -0.5, 0.25, ((0, 32),))
    conv_weight = gaussian(keys[6], (KSIZE, KSIZE, D), (KSIZE * KSIZE) ** -0.5, 0.875, (), jnp.float32)
    ln_gain = jnp.clip(1.0 + 0.15 * jax.random.normal(keys[7], (D,), jnp.float32), 0.25, 1.75)
    proj = gaussian(keys[8], (D, D), D ** -0.5, 0.1875)
    layer_scale = jnp.clip(1.0 + 0.15 * jax.random.normal(keys[9], (D,), jnp.float32), 0.25, 1.75)
    return {"tokens": tokens, "slot_keys": slot_keys, "norm_gain": norm_gain, "slot_gain": slot_gain, "w_in": w_in, "w_out": w_out, "conv_weight": conv_weight, "ln_gain": ln_gain, "proj": proj, "layer_scale": layer_scale}


def rms_scale(value, gain):
    return value * lax.rsqrt(lax.optimization_barrier(jnp.mean(value * value, axis=-1, keepdims=True)) + 1e-06) * gain

def reference(tokens, slot_keys, norm_gain, slot_gain, w_in, w_out, conv_weight, ln_gain, proj, layer_scale):
    members = tokens.shape[0]
    flat = tokens.reshape(members, ROWS * COLS, D)

    def dispatch_one(cells):
        normed = rms_scale(cells.astype(jnp.float32), norm_gain).astype(jnp.bfloat16)
        logits = jnp.dot(normed, slot_keys, preferred_element_type=jnp.float32)
        peak = lax.optimization_barrier(jnp.max(logits, axis=0))
        shifted = jnp.exp(logits - peak)
        dispatch = shifted.astype(jnp.bfloat16)
        numer = jnp.dot(dispatch.T, cells, preferred_element_type=jnp.float32)
        slot_in = rms_scale(numer, slot_gain).astype(jnp.bfloat16)
        return (slot_in, logits)
    slot_in, logits = lax.map(dispatch_one, flat)
    grouped = slot_in.reshape(members, EXPERTS, SLOTS_EXP, D).astype(jnp.float32)
    hidden = jax.nn.gelu(jnp.einsum('mesd,edf->mesf', grouped, w_in.astype(jnp.float32))).astype(jnp.bfloat16)
    slot_out = jnp.einsum('mesf,efd->mesd', hidden.astype(jnp.float32), w_out.astype(jnp.float32)).astype(jnp.bfloat16)
    slot_out = slot_out.reshape(members, SLOTS, D)

    def block_one(packed):
        cells, member_logits, outputs = packed
        combine = jax.nn.softmax(member_logits, axis=-1).astype(jnp.bfloat16)
        mixed = jnp.dot(combine, outputs, preferred_element_type=jnp.float32)
        state = (cells.astype(jnp.float32) + mixed).astype(jnp.bfloat16).reshape(ROWS, COLS, D)
        padded = jnp.pad(state, ((3, 3), (0, 0), (0, 0)))
        padded = jnp.concatenate([padded[:, COLS - 3:], padded, padded[:, :3]], axis=1)
        conv = jnp.zeros((ROWS, COLS, D), jnp.float32)
        for row_tap in range(KSIZE):
            for col_tap in range(KSIZE):
                conv = conv + padded[row_tap:row_tap + ROWS, col_tap:col_tap + COLS].astype(jnp.float32) * conv_weight[row_tap, col_tap]
        center = conv - lax.optimization_barrier(jnp.mean(conv, axis=-1, keepdims=True))
        spread = lax.optimization_barrier(jnp.mean(center * center, axis=-1, keepdims=True))
        normal = (center * lax.rsqrt(spread + 1e-06) * ln_gain).astype(jnp.bfloat16)
        branch = jnp.dot(normal.reshape(ROWS * COLS, D), proj, preferred_element_type=jnp.float32)
        result = state.reshape(ROWS * COLS, D).astype(jnp.float32) + layer_scale * jax.nn.gelu(branch)
        return result.astype(jnp.bfloat16).reshape(ROWS, COLS, D)
    return lax.map(block_one, (flat, logits, slot_out))
```

```python
import functools

import jax
import jax.numpy as jnp
from jax import lax
from jax.experimental import pallas as pl
from jax.experimental.pallas import tpu as pltpu
from jax.sharding import PartitionSpec as P

F32 = jnp.float32
BF16 = jnp.bfloat16
LANES = 128
EPS = 1e-06
MIB = 1024 * 1024
NT = (((1,), (1,)), ((), ()))
VMEM = pl.BlockSpec(memory_space=pltpu.VMEM)
SMEM = pl.BlockSpec(memory_space=pltpu.SMEM)


def dot_nt(left, right):
    return lax.dot_general(left, right, NT, preferred_element_type=F32)


def rms_scale(value, gain):
    return value * lax.rsqrt(jnp.mean(value * value, axis=-1, keepdims=True) + EPS) * gain


def cost(flops, moved, exps=0):
    return pl.CostEstimate(flops=flops, bytes_accessed=moved, transcendentals=exps)


def dispatch_kernel(layout, index_ref, cells_ref, keys_ref, gain_ref, keys_out, *rest):
    count_z, count_tok, slot_dev = layout
    outs, normed_ref = rest[:-1], rest[-1]
    total, width = cells_ref.shape
    slots = keys_ref.shape[1]
    my_z, my_tok = index_ref[0], index_ref[1]
    place = lax.broadcasted_iota(jnp.int32, (slots, slots), 0)
    source = lax.broadcasted_iota(jnp.int32, (slots, slots), 1)
    inner = lax.rem(place, slot_dev)
    core = lax.rem(place // slot_dev, 2)
    step_z = lax.rem(place // (2 * slot_dev), count_z)
    step_tok = place // (2 * slot_dev * count_z)
    at_z = lax.rem(step_z + my_z, count_z)
    at_tok = lax.rem(step_tok + my_tok, count_tok)
    wanted = ((at_z * 2 + core) * count_tok + at_tok) * slot_dev + inner
    pick = jnp.where(wanted == source, 1.0, 0.0).astype(BF16)
    keys_out[...] = dot_nt(pick, keys_ref[...]).astype(BF16)

    block = 128

    @pl.loop(0, total // block)
    def _(step):
        rows = pl.ds(pl.multiple_of(step * block, block), block)
        normed_ref[rows, :] = rms_scale(cells_ref[rows, :].astype(F32), gain_ref[...]).astype(BF16)

    part = slots // count_tok
    for at, out in enumerate(outs):
        logits = dot_nt(keys_out[at * part : (at + 1) * part, :], normed_ref[...])
        peak = jnp.max(logits, axis=1, keepdims=True)
        weight = jnp.exp(logits - peak).astype(BF16)
        out[:, :width] = jnp.dot(weight, cells_ref[...], preferred_element_type=F32).astype(BF16)
        first = peak.astype(BF16).astype(F32)
        second = (peak - first).astype(BF16).astype(F32)
        third = peak - first - second
        lane = lax.broadcasted_iota(jnp.int32, (part, LANES), 1)
        out[:, width:] = jnp.where(
            lane == 0, first, jnp.where(lane == 1, second, jnp.where(lane == 2, third, 0.0))
        ).astype(BF16)


def dispatch(index, cells, keys, gain, layout):
    count_z, count_tok, slot_dev = layout
    total, width = cells.shape
    slots = keys.shape[1]
    part = slots // count_tok
    return pl.pallas_call(
        functools.partial(dispatch_kernel, layout),
        out_shape=[jax.ShapeDtypeStruct((slots, width), BF16)]
        + [jax.ShapeDtypeStruct((part, width + LANES), BF16)] * count_tok,
        in_specs=[SMEM, VMEM, VMEM, VMEM],
        out_specs=[VMEM] * (1 + count_tok),
        scratch_shapes=[pltpu.VMEM((total, width), BF16)],
        compiler_params=pltpu.CompilerParams(vmem_limit_bytes=48 * MIB),
        cost_estimate=cost(4 * total * width * slots, 4 * total * width, total * slots),
        name="dispatch",
    )(index, cells, keys, gain)


def gather_kernel(count_z, gain_ref, *refs):
    count = len(refs) - count_z
    parts, outs = refs[:count], refs[count:]
    width = gain_ref.shape[1]
    peaks = []
    for ref in parts:
        piece = ref[:, width:].astype(F32)
        peaks.append(jnp.sum(piece, axis=1, keepdims=True))
    peak = functools.reduce(jnp.maximum, peaks)
    numer = None
    for ref, own in zip(parts, peaks):
        term = ref[:, :width].astype(F32) * jnp.exp(own - peak)
        numer = term if numer is None else numer + term
    value = rms_scale(numer, gain_ref[...]).astype(BF16)
    rows = value.shape[0] // count_z
    for at, out in enumerate(outs):
        out[...] = value[at * rows : (at + 1) * rows, :]


def gather_slots(parts, gain, count_z):
    rows, width = parts[0].shape[0] // count_z, gain.shape[1]
    return pl.pallas_call(
        functools.partial(gather_kernel, count_z),
        out_shape=[jax.ShapeDtypeStruct((rows, width), BF16)] * count_z,
        in_specs=[VMEM] * (1 + len(parts)),
        out_specs=[VMEM] * count_z,
        compiler_params=pltpu.CompilerParams(vmem_limit_bytes=32 * MIB),
        cost_estimate=cost(8 * len(parts) * rows * count_z * width, 4 * rows * count_z * width),
        name="gather_slots",
    )(gain, *parts)


def expert_kernel(count_z, slots_exp, core_ref, in_a, in_b, out_a, out_b, *refs):
    parts, outs, rows_ref, sum_ref = refs[:count_z], refs[count_z : 2 * count_z], refs[-2], refs[-1]
    each = parts[0].shape[0]
    step = pl.program_id(0)
    per_core = pl.num_programs(0)

    @pl.when(step == 0)
    def _():
        for at, ref in enumerate(parts):
            rows_ref[at * each : (at + 1) * each, :] = ref[...]
        sum_ref[...] = jnp.zeros_like(sum_ref)

    rows = rows_ref[...]
    place = lax.broadcasted_iota(jnp.int32, (rows.shape[0], 1), 0)
    expert = lax.rem(place, each) // slots_exp
    core = core_ref[0]
    for held, (w_in, w_out) in ((core, (in_a, out_a)), (1 - core, (in_b, out_b))):
        mine = expert == held * per_core + step
        hidden = jax.nn.gelu(jnp.dot(rows, w_in[0], preferred_element_type=F32))
        hidden = jnp.where(mine, hidden, 0.0).astype(BF16)
        sum_ref[...] += jnp.dot(hidden, w_out[0], preferred_element_type=F32)

    @pl.when(step == per_core - 1)
    def _():
        for at, out in enumerate(outs):
            out[...] = sum_ref[at * each : (at + 1) * each, :].astype(BF16)


def experts(core, parts, w_in, w_out, in_other, out_other, slots_exp):
    count_z = len(parts)
    each, width = parts[0].shape
    per_core, _, inner = w_in.shape
    whole = pl.BlockSpec((each, width), lambda i: (0, 0))
    spec_in = pl.BlockSpec((1, width, inner), lambda i: (i, 0, 0))
    spec_out = pl.BlockSpec((1, inner, width), lambda i: (i, 0, 0))
    rows = each * count_z
    return pl.pallas_call(
        functools.partial(expert_kernel, count_z, slots_exp),
        out_shape=[jax.ShapeDtypeStruct((each, width), BF16)] * count_z,
        grid=(per_core,),
        in_specs=[SMEM, spec_in, spec_in, spec_out, spec_out] + [whole] * count_z,
        out_specs=[whole] * count_z,
        scratch_shapes=[pltpu.VMEM((rows, width), BF16), pltpu.VMEM((rows, width), F32)],
        compiler_params=pltpu.CompilerParams(vmem_limit_bytes=40 * MIB),
        cost_estimate=cost(8 * rows * width * inner * per_core, 8 * width * inner * per_core),
        name="experts",
    )(core, w_in, in_other, w_out, out_other, *parts)


def combine_kernel(valid_ref, cells_ref, keys_ref, gain_ref, out_ref):
    normed = rms_scale(cells_ref[...].astype(F32), gain_ref[...]).astype(BF16)
    logits = dot_nt(normed, keys_ref[...])
    raised = jnp.exp(logits - jnp.max(logits, axis=-1, keepdims=True))
    share = raised * (1.0 / jnp.sum(raised, axis=-1, keepdims=True))
    out_ref[...] = jnp.where(valid_ref[0] > 0, share, 0.0).astype(BF16)


def combine_weights(valid, cells, keys, gain):
    total, width = cells.shape
    slots = keys.shape[0]
    block = 128
    return pl.pallas_call(
        combine_kernel,
        out_shape=jax.ShapeDtypeStruct((total, slots), BF16),
        grid=(total // block,),
        in_specs=[
            SMEM,
            pl.BlockSpec((block, width), lambda i: (i, 0)),
            pl.BlockSpec((slots, width), lambda i: (0, 0)),
            pl.BlockSpec((1, width), lambda i: (0, 0)),
        ],
        out_specs=pl.BlockSpec((block, slots), lambda i: (i, 0)),
        compiler_params=pltpu.CompilerParams(vmem_limit_bytes=40 * MIB),
        cost_estimate=cost(2 * total * width * slots, 2 * total * width, total * slots),
        name="combine_weights",
    )(valid, cells, keys, gain)


LEFT = 8


def block_kernel(
    dims, cells_ref, low_ref, high_ref, share_ref, share_low, share_high, weight_ref, ln_ref,
    proj_ref, scale_ref, *rest
):
    rows, cols, taps = dims
    slot_refs, out_ref = rest[:-5], rest[-5]
    slots_ref, state_ref, conv_ref, normal_ref = rest[-4:]
    reach = taps // 2
    width = cells_ref.shape[1]
    groups = width // LANES
    start = 0
    for ref in slot_refs:
        slots_ref[start : start + ref.shape[0], :] = ref[...]
        start += ref.shape[0]

    chunk = 2 * LANES

    def mix(cells, share, at, to):
        at = pl.multiple_of(at * cols, cols)
        picked = share[pl.ds(at, cols), :]
        for lane in range(0, width, chunk):
            mixed = jnp.dot(picked, slots_ref[:, lane : lane + chunk], preferred_element_type=F32)
            value = cells[pl.ds(at, cols), lane : lane + chunk].astype(F32) + mixed
            value = value.astype(BF16).astype(F32)
            for half in range(chunk // LANES):
                group = lane // LANES + half
                piece = value[:, half * LANES : (half + 1) * LANES]
                state_ref[group, to, LEFT : LEFT + cols, :] = piece
                state_ref[group, to, 0:LEFT, :] = piece[cols - LEFT :, :]
                state_ref[group, to, LEFT + cols : 2 * LEFT + cols, :] = piece[:LEFT, :]

    @pl.loop(0, reach)
    def _(row):
        mix(low_ref, share_low, row, row)

    @pl.loop(0, rows)
    def _(row):
        mix(cells_ref, share_ref, row, row + reach)

    @pl.loop(0, reach)
    def _(row):
        mix(high_ref, share_high, row, row + rows + reach)

    span = 16

    @pl.loop(0, groups)
    def _(group):
        lanes = pl.ds(pl.multiple_of(group * LANES, LANES), LANES)

        @pl.loop(0, cols // span)
        def _(piece):
            base = pl.multiple_of(piece * span, span)
            for first in range(0, rows, 8):
                sums = [[None] * (span // 8) for _ in range(8)]
                for col_tap in range(taps):
                    weights = [
                        jnp.broadcast_to(weight_ref[row_tap, col_tap : col_tap + 1, lanes], (8, LANES))
                        for row_tap in range(taps)
                    ]
                    for row in range(8 + taps - 1):
                        for part in range(span // 8):
                            value = state_ref[
                                group,
                                first + row,
                                pl.ds(base + (part * 8 + LEFT - reach + col_tap), 8),
                                :,
                            ]
                            for out_row in range(max(0, row - taps + 1), min(8, row + 1)):
                                term = value * weights[row - out_row]
                                have = sums[out_row][part]
                                sums[out_row][part] = term if have is None else have + term
                for out_row in range(8):
                    for part in range(span // 8):
                        conv_ref[
                            group, pl.ds((first + out_row) * cols + base + part * 8, 8), :
                        ] = sums[out_row][part]

    block = 64

    @pl.loop(0, rows * cols // block)
    def _(step):
        at = pl.ds(pl.multiple_of(step * block, block), block)
        values = [conv_ref[group, at, :] for group in range(groups)]
        mean = jnp.sum(sum(values), axis=-1, keepdims=True) * (1.0 / width)
        centers = [value - mean for value in values]
        spread = jnp.sum(sum(c * c for c in centers), axis=-1, keepdims=True) * (1.0 / width)
        factor = lax.rsqrt(spread + EPS)
        for group in range(groups):
            lanes = slice(group * LANES, (group + 1) * LANES)
            normal_ref[at, lanes] = (centers[group] * factor * ln_ref[:, lanes]).astype(BF16)

    @pl.loop(0, rows)
    def _(row):
        at = pl.ds(pl.multiple_of(row * cols, cols), cols)
        for lane in range(0, width, chunk):
            branch = jnp.dot(
                normal_ref[at, :], proj_ref[:, lane : lane + chunk], preferred_element_type=F32
            )
            branch = scale_ref[:, lane : lane + chunk] * jax.nn.gelu(branch)
            for half in range(chunk // LANES):
                group = lane // LANES + half
                state = state_ref[group, row + reach, LEFT : LEFT + cols, :]
                out_ref[at, group * LANES : (group + 1) * LANES] = (
                    state + branch[:, half * LANES : (half + 1) * LANES]
                ).astype(BF16)


def block_fields(dims, cells, halo, shares, weight, ln_gain, proj, scale, slot_parts):
    rows, cols, taps = dims
    total, width = cells.shape
    slots = sum(part.shape[0] for part in slot_parts)
    groups = width // LANES
    padded = rows + taps - 1
    return pl.pallas_call(
        functools.partial(block_kernel, dims),
        out_shape=jax.ShapeDtypeStruct((total, width), BF16),
        in_specs=[VMEM] * (10 + len(slot_parts)),
        out_specs=VMEM,
        scratch_shapes=[
            pltpu.VMEM((slots, width), BF16),
            pltpu.VMEM((groups, padded, cols + 2 * LEFT, LANES), F32),
            pltpu.VMEM((groups, total, LANES), F32),
            pltpu.VMEM((total, width), BF16),
        ],
        compiler_params=pltpu.CompilerParams(vmem_limit_bytes=48 * MIB),
        cost_estimate=cost(4 * total * width * width, 8 * total * width, total * width),
        name="block_fields",
    )(cells, *halo, *shares, weight, ln_gain, proj, scale, *slot_parts)


def local(
    tokens, slot_keys, norm_gain, slot_gain, w_in, w_out, conv_weight, ln_gain, proj, layer_scale
):
    rows, cols, width = tokens.shape[1:]
    count_fc = lax.axis_size("fc")
    count_tok = lax.axis_size("tok")
    count_z = count_fc // 2
    slots = slot_keys.shape[1]
    slot_dev = slots // (count_fc * count_tok)
    slots_exp = slot_dev // w_in.shape[0]
    taps = conv_weight.shape[0]
    reach = taps // 2
    at_fc, at_tok = lax.axis_index("fc"), lax.axis_index("tok")
    cells = tokens.reshape(rows * cols, width)
    norm_gain, slot_gain = norm_gain.reshape(1, width), slot_gain.reshape(1, width)
    ln_gain, layer_scale = ln_gain.reshape(1, width), layer_scale.reshape(1, width)

    def shift(value, axis, step):
        count = lax.axis_size(axis)
        return lax.ppermute(value, axis, [(i, (i + step) % count) for i in range(count)])

    other = [(i, i ^ 1) for i in range(count_fc)]
    in_other = lax.ppermute(w_in, "fc", other)
    out_other = lax.ppermute(w_out, "fc", other)

    index = jnp.stack([at_fc // 2, at_tok]).astype(jnp.int32)
    keys, *numer = dispatch(index, cells, slot_keys, norm_gain, (count_z, count_tok, slot_dev))
    parts = [numer[0]] + [shift(numer[k], "tok", k) for k in range(1, count_tok)]

    forward = [(i, i + 1) for i in range(count_tok - 1)]
    backward = [(i + 1, i) for i in range(count_tok - 1)]
    low = lax.ppermute(cells[(rows - reach) * cols :], "tok", forward)
    high = lax.ppermute(cells[: reach * cols], "tok", backward)
    always = jnp.ones((1,), jnp.int32)
    has_low = (at_tok > 0).astype(jnp.int32).reshape(1)
    has_high = (at_tok < count_tok - 1).astype(jnp.int32).reshape(1)
    share = combine_weights(always, cells, keys, norm_gain)
    share_low = combine_weights(has_low, low, keys, norm_gain)
    share_high = combine_weights(has_high, high, keys, norm_gain)

    slot_in = gather_slots(parts, slot_gain, count_z)
    arrived = [slot_in[0]] + [shift(slot_in[k], "fc", 2 * k) for k in range(1, count_z)]
    core = (at_fc % 2).astype(jnp.int32).reshape(1)
    made = experts(core, arrived, w_in, w_out, in_other, out_other, slots_exp)
    back = [made[0]] + [shift(made[k], "fc", -2 * k) for k in range(1, count_z)]
    mine = jnp.concatenate(back, axis=0)
    every = [mine] + [shift(mine, "tok", -k) for k in range(1, count_tok)]

    fields = block_fields(
        (rows, cols, taps), cells, (low, high), (share, share_low, share_high), conv_weight,
        ln_gain, proj, layer_scale, every,
    )
    return fields.reshape(1, rows, cols, width)


def solution(mesh):
    return jax.shard_map(
        local,
        mesh=mesh,
        in_specs=(
            P("fc", "tok", None, None),
            P(),
            P(),
            P(),
            P(("fc", "tok"), None, None),
            P(("fc", "tok"), None, None),
            P(),
            P(),
            P(),
            P(),
        ),
        out_specs=P("fc", "tok", None, None),
        check_vma=False,
    )
```

```python
import functools

import jax
import jax.numpy as jnp
import ml_dtypes
import numpy as np
from jax import lax
from jax.experimental import pallas as pl
from jax.experimental.pallas import tpu as pltpu
from jax.sharding import PartitionSpec as P

F32 = jnp.float32
BF16 = jnp.bfloat16
LANES = 128
EPS = 1e-06
MIB = 1024 * 1024
LIMIT_D = 16
LIMIT_E = 16
NT = (((1,), (1,)), ((), ()))
VMEM = pl.BlockSpec(memory_space=pltpu.VMEM)
SMEM = pl.BlockSpec(memory_space=pltpu.SMEM)
HBM = pl.BlockSpec(memory_space=pltpu.HBM)
ANY = pl.BlockSpec(memory_space=pl.ANY)


def dot_nt(left, right):
    return lax.dot_general(left, right, NT, preferred_element_type=F32)


def rms_scale(value, gain):
    return value * lax.rsqrt(jnp.mean(value * value, axis=-1, keepdims=True) + EPS) * gain


def split_index(value, count):
    if count & (count - 1) == 0:
        return value >> (count.bit_length() - 1), value & (count - 1)
    return value // count, lax.rem(value, count)


def cost(flops, moved, exps=0):
    return pl.CostEstimate(flops=flops, bytes_accessed=moved, transcendentals=exps)


def dispatch_kernel(layout, index_ref, cells_hbm, keys_hbm, gain_ref, keys_out, *rest):
    count_z, count_tok, slot_dev = layout
    outs, (cells_ref, keys_ref, normed_ref, cell_sems, key_sem) = rest[:-5], rest[-5:]
    total, width = cells_ref.shape
    slots = keys_ref.shape[1]
    my_z, my_tok = index_ref[0], index_ref[1]
    count = cell_sems.shape[0]
    block = total // count
    key_copy = pltpu.make_async_copy(keys_hbm, keys_ref, key_sem)
    key_copy.start()
    copies = []
    for step in range(count):
        rows = slice(step * block, (step + 1) * block)
        copies.append(
            pltpu.make_async_copy(cells_hbm.at[rows], cells_ref.at[rows], cell_sems.at[step])
        )
        copies[-1].start()
    place = lax.broadcasted_iota(jnp.int32, (slots, 1), 0)
    source = lax.broadcasted_iota(jnp.int32, (slots, slots), 1)
    outer, inner = split_index(place, slot_dev)
    outer, core = split_index(outer, 2)
    step_tok, step_z = split_index(outer, count_z)
    at_z = split_index(step_z + my_z, count_z)[1]
    at_tok = split_index(step_tok + my_tok, count_tok)[1]
    wanted = ((at_z * 2 + core) * count_tok + at_tok) * slot_dev + inner
    pick = jnp.where(wanted == source, 1.0, 0.0).astype(BF16)
    key_copy.wait()
    keys = dot_nt(pick, keys_ref[...]).astype(BF16)
    keys_out[...] = keys

    for step in range(count):
        rows = slice(step * block, (step + 1) * block)
        copies[step].wait()
        normed_ref[rows, :] = rms_scale(cells_ref[rows, :].astype(F32), gain_ref[...]).astype(BF16)

    part = slots // count_tok
    logits = dot_nt(keys, normed_ref[...])
    peak = jnp.max(logits, axis=1, keepdims=True)
    weight = jnp.exp(logits - peak).astype(BF16)
    first = peak.astype(BF16).astype(F32)
    second = (peak - first).astype(BF16).astype(F32)
    third = peak - first - second
    lane = lax.broadcasted_iota(jnp.int32, (slots, LANES), 1)
    marks = jnp.where(
        lane == 0, first, jnp.where(lane == 1, second, jnp.where(lane == 2, third, 0.0))
    ).astype(BF16)
    for at, out in enumerate(outs):
        out[:, width:] = marks[at * part : (at + 1) * part, :]
    for lane in range(0, width, 2 * LANES):
        lanes = slice(lane, lane + 2 * LANES)
        numer = jnp.dot(weight, cells_ref[:, lanes], preferred_element_type=F32).astype(BF16)
        for at, out in enumerate(outs):
            out[:, lanes] = numer[at * part : (at + 1) * part, :]


def dispatch(index, cells, keys, gain, layout):
    count_z, count_tok, slot_dev = layout
    total, width = cells.shape
    slots = keys.shape[1]
    part = slots // count_tok
    count = 8
    return pl.pallas_call(
        functools.partial(dispatch_kernel, layout),
        out_shape=[jax.ShapeDtypeStruct((slots, width), BF16)]
        + [jax.ShapeDtypeStruct((part, width + LANES), BF16)] * count_tok,
        in_specs=[SMEM, HBM, HBM, VMEM],
        out_specs=[VMEM] * (1 + count_tok),
        scratch_shapes=[
            pltpu.VMEM((total, width), BF16),
            pltpu.VMEM((width, slots), BF16),
            pltpu.VMEM((total, width), BF16),
            pltpu.SemaphoreType.DMA((count,)),
            pltpu.SemaphoreType.DMA,
        ],
        compiler_params=pltpu.CompilerParams(vmem_limit_bytes=LIMIT_D * MIB),
        cost_estimate=cost(4 * total * width * slots, 4 * total * width, total * slots),
        name="dispatch",
    )(index, cells, keys, gain)


def gather_kernel(count_z, gain_ref, *refs):
    count = len(refs) - count_z
    parts, outs = refs[:count], refs[count:]
    width = gain_ref.shape[1]
    peaks = []
    for ref in parts:
        piece = ref[:, width:].astype(F32)
        peaks.append(jnp.sum(piece, axis=1, keepdims=True))
    peak = functools.reduce(jnp.maximum, peaks)
    numer = None
    for ref, own in zip(parts, peaks):
        term = ref[:, :width].astype(F32) * jnp.exp(own - peak)
        numer = term if numer is None else numer + term
    value = rms_scale(numer, gain_ref[...]).astype(BF16)
    rows = value.shape[0] // count_z
    for at, out in enumerate(outs):
        out[...] = value[at * rows : (at + 1) * rows, :]


def gather_slots(parts, gain, count_z):
    rows, width = parts[0].shape[0] // count_z, gain.shape[1]
    return pl.pallas_call(
        functools.partial(gather_kernel, count_z),
        out_shape=[jax.ShapeDtypeStruct((rows, width), BF16)] * count_z,
        in_specs=[VMEM] * (1 + len(parts)),
        out_specs=[VMEM] * count_z,
        compiler_params=pltpu.CompilerParams(vmem_limit_bytes=8 * MIB),
        cost_estimate=cost(8 * len(parts) * rows * count_z * width, 4 * rows * count_z * width),
        name="gather_slots",
    )(gain, *parts)


def expert_kernel(count_z, slots_exp, core_ref, _, in_own, out_own, in_other, out_other, *refs):
    parts, outs = refs[:count_z], refs[count_z : 2 * count_z]
    rows_ref, sum_ref, in_ref, out_ref, sems = refs[2 * count_z :]
    each = parts[0].shape[0]
    per_core = in_own.shape[0]
    copies = []
    for which, pair in enumerate(((in_own, out_own), (in_other, out_other))):
        for at in range(per_core):
            place = which * per_core + at
            for kind, (source, target) in enumerate(zip(pair, (in_ref, out_ref))):
                copies.append(
                    pltpu.make_async_copy(
                        source.at[at], target.at[place], sems.at[2 * place + kind]
                    )
                )
                copies[-1].start()
    for at, ref in enumerate(parts):
        rows_ref[at * each : (at + 1) * each, :] = ref[...]
    rows = rows_ref[...]
    place = lax.broadcasted_iota(jnp.int32, (rows.shape[0], 1), 0)
    expert = lax.rem(place, each) // slots_exp
    core = core_ref[0]

    for at in range(2 * per_core):
        held = core if at < per_core else 1 - core
        mine = expert == held * per_core + at % per_core
        copies[2 * at].wait()
        hidden = jax.nn.gelu(jnp.dot(rows, in_ref[at], preferred_element_type=F32))
        hidden = jnp.where(mine, hidden, 0.0).astype(BF16)
        copies[2 * at + 1].wait()
        made = jnp.dot(hidden, out_ref[at], preferred_element_type=F32)
        if at == 0:
            sum_ref[...] = made
        else:
            sum_ref[...] += made
    for at, out in enumerate(outs):
        out[...] = sum_ref[at * each : (at + 1) * each, :].astype(BF16)


def experts(core, after, parts, w_in, w_out, in_other, out_other, slots_exp):
    count_z = len(parts)
    each, width = parts[0].shape
    per_core, _, inner = w_in.shape
    rows = each * count_z
    return pl.pallas_call(
        functools.partial(expert_kernel, count_z, slots_exp),
        out_shape=[jax.ShapeDtypeStruct((each, width), BF16)] * count_z,
        in_specs=[SMEM, ANY, HBM, HBM, HBM, HBM] + [VMEM] * count_z,
        out_specs=[VMEM] * count_z,
        scratch_shapes=[
            pltpu.VMEM((rows, width), BF16),
            pltpu.VMEM((rows, width), F32),
            pltpu.VMEM((2 * per_core, width, inner), BF16),
            pltpu.VMEM((2 * per_core, inner, width), BF16),
            pltpu.SemaphoreType.DMA((4 * per_core,)),
        ],
        compiler_params=pltpu.CompilerParams(vmem_limit_bytes=LIMIT_E * MIB),
        cost_estimate=cost(8 * rows * width * inner * per_core, 8 * width * inner * per_core),
        name="experts",
    )(core, after, w_in, w_out, in_other, out_other, *parts)


def copy_kernel(start_ref, cells_ref, _, out_ref):
    rows = out_ref.shape[0]
    out_ref[...] = cells_ref[pl.ds(pl.multiple_of(start_ref[0], LANES), rows), :]


def edge_rows(start, cells, rows, after):
    return pl.pallas_call(
        copy_kernel,
        out_shape=jax.ShapeDtypeStruct((rows, cells.shape[1]), BF16),
        in_specs=[SMEM, VMEM, ANY],
        out_specs=VMEM,
        compiler_params=pltpu.CompilerParams(vmem_limit_bytes=8 * MIB),
        cost_estimate=cost(0, 4 * rows * cells.shape[1]),
        name="edge_rows",
    )(start, cells, after)


def combine_kernel(count, valid_ref, keys_ref, gain_ref, _, *refs):
    block = 128
    for at, (cells_ref, out_ref) in enumerate(zip(refs[:count], refs[count:])):
        for start in range(0, cells_ref.shape[0], block):
            rows = slice(start, start + block)
            normed = rms_scale(cells_ref[rows, :].astype(F32), gain_ref[...]).astype(BF16)
            logits = dot_nt(normed, keys_ref[...])
            raised = jnp.exp(logits - jnp.max(logits, axis=-1, keepdims=True))
            share = raised * (1.0 / jnp.sum(raised, axis=-1, keepdims=True))
            out_ref[rows, :] = jnp.where(valid_ref[at] > 0, share, 0.0).astype(BF16)


def combine_weights(valid, cells, keys, gain, after):
    width, slots = gain.shape[1], keys.shape[0]
    total = sum(part.shape[0] for part in cells)
    return pl.pallas_call(
        functools.partial(combine_kernel, len(cells)),
        out_shape=[jax.ShapeDtypeStruct((part.shape[0], slots), BF16) for part in cells],
        in_specs=[SMEM, VMEM, VMEM, ANY] + [VMEM] * len(cells),
        out_specs=[VMEM] * len(cells),
        compiler_params=pltpu.CompilerParams(vmem_limit_bytes=16 * MIB),
        cost_estimate=cost(2 * total * width * slots, 2 * total * width, total * slots),
        name="combine_weights",
    )(valid, keys, gain, after, *cells)


def pieces(value, count):
    out = []
    for _ in range(count):
        piece = value.astype(BF16)
        out.append(piece)
        value = value - piece.astype(value.dtype)
    return out


def wave(cols, taps):
    half = cols // 2
    freq = np.arange(half)[:, None]
    angle = 2 * np.pi * ((freq * np.arange(cols)[None, :]) % cols) / cols
    sign = np.where(np.arange(cols) % 2 == 0, 1.0, -1.0)
    real, imag = np.cos(angle), -np.sin(angle)
    imag[0] = sign
    to_freq = np.concatenate([real, imag], axis=0)
    back_real, back_imag = 2 * np.cos(angle).T / cols, -2 * np.sin(angle).T / cols
    back_real[:, 0] = sign / cols
    back_imag[:, 0] = 1 / cols
    to_cols = np.concatenate([back_real, back_imag], axis=1)
    offset = np.arange(taps) - taps // 2
    turn = 2 * np.pi * freq * offset[None, :] / cols
    first, second, third = np.cos(turn), np.sin(turn) - np.cos(turn), np.sin(turn) + np.cos(turn)
    first[0], second[0] = 0.0, 1.0
    third[0] = np.where(offset % 2 == 0, -1.0, 1.0)
    spectrum = np.zeros((3 * half, 8))
    spectrum[:, :taps] = np.concatenate([first, second, third], axis=0)

    def split(value):
        high = value.astype(np.float32).astype(ml_dtypes.bfloat16)
        return high, (value - high.astype(np.float64)).astype(np.float32).astype(ml_dtypes.bfloat16)

    f_high, f_low = split(to_freq)
    c_high, c_low = split(to_cols)
    s_high, s_low = split(spectrum)
    return (
        np.concatenate([f_high, f_low], axis=1),
        np.concatenate([c_high, c_high], axis=1),
        c_low,
        np.concatenate([s_high, s_high, s_high, s_low, s_low], axis=1),
    )


def fill_spectrum(coef_ref, weight_ref, out_ref):
    taps, _, width = weight_ref.shape
    fill = jnp.zeros((8 - taps, width), F32)
    for tap in range(taps):
        row = jnp.concatenate([weight_ref[tap], fill], axis=0)
        one, two, three = (p.astype(F32) for p in pieces(row, 3))
        stack = jnp.concatenate([one, two, three, one, two], axis=0).astype(BF16)
        out_ref[tap] = jnp.dot(coef_ref[...], stack, preferred_element_type=F32)


def block_kernel(
    dims, place_ref, cells_ref, low_ref, high_ref, share_ref, share_low, share_high, weight_ref, freq_ref,
    cols_ref, fine_ref, coef_ref, ln_ref, proj_ref, scale_ref, *rest
):
    rows, cols, taps = dims
    slot_refs, out_ref = rest[:-7], rest[-7]
    slots_ref, state_ref, freqs_ref, back_ref, conv_ref, spectrum_ref = rest[-6:]
    reach = taps // 2
    half = cols // 2
    width = cells_ref.shape[1]
    start = 0
    for ref in slot_refs:
        slots_ref[start : start + ref.shape[0], :] = ref[...]
        start += ref.shape[0]
    fill_spectrum(coef_ref, weight_ref, spectrum_ref)

    chunk = 2 * LANES

    def mix(cells, share, row, to, keep):
        at = pl.ds(pl.multiple_of(row * cols, cols), cols)
        picked = share[at, :]
        for lane in range(0, width, chunk):
            lanes = slice(lane, lane + chunk)
            mixed = jnp.dot(picked, slots_ref[:, lanes], preferred_element_type=F32)
            state = (cells[at, lanes].astype(F32) + mixed).astype(BF16)
            if keep:
                state_ref[at, lanes] = state
            twice = jnp.concatenate([state, state], axis=0)
            freqs_ref[to, :, lanes] = jnp.dot(freq_ref[...], twice, preferred_element_type=F32)

    @pl.loop(0, reach)
    def _(row):
        mix(low_ref, share_low, row, row + place_ref[0], False)
        mix(high_ref, share_high, row, row + place_ref[1], False)

    @pl.loop(0, rows)
    def _(row):
        mix(cells_ref, share_ref, row, row + reach, True)

    tile = 16

    @pl.loop(0, width // LANES)
    def _(group):
        lanes = pl.ds(pl.multiple_of(group * LANES, LANES), LANES)

        @pl.loop(0, half // tile)
        def _(step):
            base = pl.multiple_of(step * tile, tile)
            for first in range(0, rows, 8):
                parts = ([], [])
                for sub in range(0, tile, 8):
                    real_at, imag_at = pl.ds(base + sub, 8), pl.ds(base + half + sub, 8)
                    third_at = pl.ds(base + 2 * half + sub, 8)
                    weights = [
                        [spectrum_ref[tap, at, lanes] for tap in range(taps)]
                        for at in (real_at, imag_at, third_at)
                    ]
                    sums = [[None] * 8 for _ in range(3)]
                    for row in range(8 + taps - 1):
                        real = freqs_ref[first + row, real_at, lanes]
                        imag = freqs_ref[first + row, imag_at, lanes]
                        for kind, value in enumerate((real + imag, real, imag)):
                            for to in range(max(0, row - taps + 1), min(8, row + 1)):
                                term = value * weights[kind][row - to]
                                have = sums[kind][to]
                                sums[kind][to] = term if have is None else have + term
                    parts[0].append([sums[0][to] - sums[2][to] for to in range(8)])
                    parts[1].append([sums[0][to] + sums[1][to] for to in range(8)])
                for to in range(8):
                    for which in range(2):
                        value = jnp.concatenate([sub[to] for sub in parts[which]], axis=0)
                        high, low = pieces(value, 2)
                        back_ref[first + to, pl.ds(base + which * half, tile), lanes] = high
                        back_ref[first + to, pl.ds(base + cols + which * half, tile), lanes] = low

    pair = 2 if rows % 2 == 0 else 1

    @pl.loop(0, rows // pair)
    def _(step):
        for one in range(pair):
            total = None
            for lane in range(0, width, chunk):
                lanes = slice(lane, lane + chunk)
                row = step * pair + one
                conv = jnp.dot(cols_ref[...], back_ref[row, :, lanes], preferred_element_type=F32)
                conv += jnp.dot(fine_ref[...], back_ref[row, :cols, lanes], preferred_element_type=F32)
                conv_ref[one * cols : (one + 1) * cols, lanes] = conv
        at = pl.ds(pl.multiple_of(step * (pair * cols), pair * cols), pair * cols)
        conv = conv_ref[...]
        center = conv - jnp.mean(conv, axis=-1, keepdims=True)
        spread = jnp.mean(center * center, axis=-1, keepdims=True)
        normal = (center * lax.rsqrt(spread + EPS) * ln_ref[...]).astype(BF16)
        for lane in range(0, width, chunk):
            lanes = slice(lane, lane + chunk)
            branch = jnp.dot(normal, proj_ref[:, lanes], preferred_element_type=F32)
            branch = scale_ref[:, lanes] * jax.nn.gelu(branch)
            out_ref[at, lanes] = (state_ref[at, lanes].astype(F32) + branch).astype(BF16)


def block_fields(dims, places, cells, halo, shares, weight, ln_gain, proj, scale, slot_parts):
    rows, cols, taps = dims
    total, width = cells.shape
    slots = sum(part.shape[0] for part in slot_parts)
    padded = rows + taps - 1
    freq, to_cols, fine, coef = wave(cols, taps)
    return pl.pallas_call(
        functools.partial(block_kernel, dims),
        out_shape=jax.ShapeDtypeStruct((total, width), BF16),
        in_specs=[SMEM] + [VMEM] * (14 + len(slot_parts)),
        out_specs=VMEM,
        scratch_shapes=[
            pltpu.VMEM((slots, width), BF16),
            pltpu.VMEM((total, width), BF16),
            pltpu.VMEM((padded, cols, width), F32),
            pltpu.VMEM((rows, 2 * cols, width), BF16),
            pltpu.VMEM(((2 if rows % 2 == 0 else 1) * cols, width), F32),
            pltpu.VMEM((taps, coef.shape[0], width), F32),
        ],
        compiler_params=pltpu.CompilerParams(vmem_limit_bytes=32 * MIB),
        cost_estimate=cost(6 * total * width * width, 8 * total * width, total * width),
        name="block_fields",
    )(places, cells, *halo, *shares, weight, freq, to_cols, fine, coef, ln_gain, proj, scale, *slot_parts)


def local(
    tokens, slot_keys, norm_gain, slot_gain, w_in, w_out, conv_weight, ln_gain, proj, layer_scale
):
    rows, cols, width = tokens.shape[1:]
    count_fc = lax.axis_size("fc")
    count_tok = lax.axis_size("tok")
    count_z = count_fc // 2
    slots = slot_keys.shape[1]
    slot_dev = slots // (count_fc * count_tok)
    slots_exp = slot_dev // w_in.shape[0]
    taps = conv_weight.shape[0]
    reach = taps // 2
    at_fc, at_tok = lax.axis_index("fc"), lax.axis_index("tok")
    other = [(i, i ^ 1) for i in range(count_fc)]
    cells = tokens.reshape(rows * cols, width)
    norm_gain, slot_gain = norm_gain.reshape(1, width), slot_gain.reshape(1, width)
    ln_gain, layer_scale = ln_gain.reshape(1, width), layer_scale.reshape(1, width)

    def shift(value, axis, step):
        count = lax.axis_size(axis)
        return lax.ppermute(value, axis, [(i, (i + step) % count) for i in range(count)])

    other = [(i, i ^ 1) for i in range(count_fc)]
    tie = lax.optimization_barrier
    even = at_tok % 2 == 0
    last = (rows - reach) * cols

    def swap(start):
        pairs = [(i, i + 1) for i in range(start, count_tok - 1, 2)]
        return pairs + [(j, i) for i, j in pairs]

    edge = lax.dynamic_slice_in_dim(cells, jnp.where(even, last, 0), reach * cols, axis=0)
    first_halo = lax.ppermute(edge, "tok", swap(0))
    in_other = lax.ppermute(w_in, "fc", other)
    out_other = lax.ppermute(w_out, "fc", other)

    index = jnp.stack([at_fc // 2, at_tok]).astype(jnp.int32)
    keys, *numer = dispatch(index, cells, slot_keys, norm_gain, (count_z, count_tok, slot_dev))
    numer[1], in_other, out_other = tie((numer[1], in_other, out_other))
    parts = [numer[0]] + [shift(numer[k], "tok", k) for k in range(1, count_tok)]

    slot_in = gather_slots(parts, slot_gain, count_z)
    arrived = [slot_in[0]] + [shift(slot_in[k], "fc", 2 * k) for k in range(1, count_z)]
    first = edge_rows(jnp.where(even, 0, last).reshape(1), cells, reach * cols, slot_in[0])
    second_halo = lax.ppermute(first, "tok", swap(1))
    always = jnp.ones((1,), jnp.int32)
    (share,) = combine_weights(always, [cells], keys, norm_gain, first)
    core = (at_fc % 2).astype(jnp.int32).reshape(1)
    made = experts(core, share, arrived, w_in, w_out, in_other, out_other, slots_exp)
    back = [made[0]] + [shift(made[k], "fc", -2 * k) for k in range(1, count_z)]
    mine = jnp.concatenate(back, axis=0)
    above, below = at_tok > 0, at_tok < count_tok - 1
    inside = jnp.stack([jnp.where(even, below, above), jnp.where(even, above, below)])
    halo = (first_halo, second_halo)
    halo_shares = combine_weights(inside.astype(jnp.int32), halo, keys, norm_gain, made[0])
    places = jnp.where(even, jnp.array([rows + reach, 0]), jnp.array([0, rows + reach]))
    every = [mine] + [shift(mine, "tok", -k) for k in range(1, count_tok)]

    fields = block_fields(
        (rows, cols, taps), places.astype(jnp.int32), cells, halo, (share, *halo_shares), conv_weight,
        ln_gain, proj, layer_scale, every,
    )
    return fields.reshape(1, rows, cols, width)


def solution(mesh):
    return jax.shard_map(
        local,
        mesh=mesh,
        in_specs=(
            P("fc", "tok", None, None),
            P(),
            P(),
            P(),
            P(("fc", "tok"), None, None),
            P(("fc", "tok"), None, None),
            P(),
            P(),
            P(),
            P(),
        ),
        out_specs=P("fc", "tok", None, None),
        check_vma=False,
    )
```

```python
import functools

import jax
import jax.numpy as jnp
import ml_dtypes
import numpy as np
from jax import lax
from jax.experimental import pallas as pl
from jax.experimental.pallas import tpu as pltpu
from jax.sharding import PartitionSpec as P

F32 = jnp.float32
BF16 = jnp.bfloat16
LANES = 128
EPS = 1e-06
MIB = 1024 * 1024
LIMIT_D = 56
LIMIT_E = 16
NT = (((1,), (1,)), ((), ()))
VMEM = pl.BlockSpec(memory_space=pltpu.VMEM)
SMEM = pl.BlockSpec(memory_space=pltpu.SMEM)
HBM = pl.BlockSpec(memory_space=pltpu.HBM)
ANY = pl.BlockSpec(memory_space=pl.ANY)


def dot_nt(left, right):
    return lax.dot_general(left, right, NT, preferred_element_type=F32)


def rms_scale(value, gain):
    return value * lax.rsqrt(jnp.mean(value * value, axis=-1, keepdims=True) + EPS) * gain


def split_index(value, count):
    if count & (count - 1) == 0:
        return value >> (count.bit_length() - 1), value & (count - 1)
    return value // count, lax.rem(value, count)


def cost(flops, moved, exps=0):
    return pl.CostEstimate(flops=flops, bytes_accessed=moved, transcendentals=exps)


def dispatch_kernel(layout, index_ref, cells_hbm, keys_hbm, gain_ref, keys_out, *rest):
    count_z, count_tok, slot_dev = layout
    outs, (cells_ref, keys_ref, normed_ref, cell_sems, key_sem) = rest[:-5], rest[-5:]
    total, width = cells_ref.shape
    slots = keys_ref.shape[1]
    my_z, my_tok = index_ref[0], index_ref[1]
    count = cell_sems.shape[0]
    block = total // count
    key_copy = pltpu.make_async_copy(keys_hbm, keys_ref, key_sem)
    key_copy.start()
    copies = []
    for step in range(count):
        rows = slice(step * block, (step + 1) * block)
        copies.append(
            pltpu.make_async_copy(cells_hbm.at[rows], cells_ref.at[rows], cell_sems.at[step])
        )
        copies[-1].start()
    place = lax.broadcasted_iota(jnp.int32, (slots, 1), 0)
    source = lax.broadcasted_iota(jnp.int32, (slots, slots), 1)
    outer, inner = split_index(place, slot_dev)
    outer, core = split_index(outer, 2)
    step_tok, step_z = split_index(outer, count_z)
    at_z = split_index(step_z + my_z, count_z)[1]
    at_tok = split_index(step_tok + my_tok, count_tok)[1]
    wanted = ((at_z * 2 + core) * count_tok + at_tok) * slot_dev + inner
    pick = jnp.where(wanted == source, 1.0, 0.0).astype(BF16)
    key_copy.wait()
    keys = dot_nt(pick, keys_ref[...]).astype(BF16)
    keys_out[...] = keys

    for step in range(count):
        rows = slice(step * block, (step + 1) * block)
        copies[step].wait()
        normed_ref[rows, :] = rms_scale(cells_ref[rows, :].astype(F32), gain_ref[...]).astype(BF16)

    part = slots // count_tok
    logits = dot_nt(keys, normed_ref[...])
    peak = jnp.max(logits, axis=1, keepdims=True)
    weight = jnp.exp(logits - peak).astype(BF16)
    first = peak.astype(BF16).astype(F32)
    second = (peak - first).astype(BF16).astype(F32)
    third = peak - first - second
    lane = lax.broadcasted_iota(jnp.int32, (slots, LANES), 1)
    marks = jnp.where(
        lane == 0, first, jnp.where(lane == 1, second, jnp.where(lane == 2, third, 0.0))
    ).astype(BF16)
    for at, out in enumerate(outs):
        out[:, width:] = marks[at * part : (at + 1) * part, :]
    for lane in range(0, width, 2 * LANES):
        lanes = slice(lane, lane + 2 * LANES)
        numer = jnp.dot(weight, cells_ref[:, lanes], preferred_element_type=F32).astype(BF16)
        for at, out in enumerate(outs):
            out[:, lanes] = numer[at * part : (at + 1) * part, :]


def dispatch(index, cells, keys, gain, layout):
    count_z, count_tok, slot_dev = layout
    total, width = cells.shape
    slots = keys.shape[1]
    part = slots // count_tok
    count = 8
    return pl.pallas_call(
        functools.partial(dispatch_kernel, layout),
        out_shape=[jax.ShapeDtypeStruct((slots, width), BF16)]
        + [jax.ShapeDtypeStruct((part, width + LANES), BF16)] * count_tok,
        in_specs=[SMEM, HBM, HBM, VMEM],
        out_specs=[VMEM] * (1 + count_tok),
        scratch_shapes=[
            pltpu.VMEM((total, width), BF16),
            pltpu.VMEM((width, slots), BF16),
            pltpu.VMEM((total, width), BF16),
            pltpu.SemaphoreType.DMA((count,)),
            pltpu.SemaphoreType.DMA,
        ],
        compiler_params=pltpu.CompilerParams(vmem_limit_bytes=LIMIT_D * MIB),
        cost_estimate=cost(4 * total * width * slots, 4 * total * width, total * slots),
        name="dispatch",
    )(index, cells, keys, gain)


def gather_kernel(count_z, gain_ref, *refs):
    count = len(refs) - count_z
    parts, outs = refs[:count], refs[count:]
    width = gain_ref.shape[1]
    peaks = []
    for ref in parts:
        piece = ref[:, width:].astype(F32)
        peaks.append(jnp.sum(piece, axis=1, keepdims=True))
    peak = functools.reduce(jnp.maximum, peaks)
    numer = None
    for ref, own in zip(parts, peaks):
        term = ref[:, :width].astype(F32) * jnp.exp(own - peak)
        numer = term if numer is None else numer + term
    value = rms_scale(numer, gain_ref[...]).astype(BF16)
    rows = value.shape[0] // count_z
    for at, out in enumerate(outs):
        out[...] = value[at * rows : (at + 1) * rows, :]


def gather_slots(parts, gain, count_z):
    rows, width = parts[0].shape[0] // count_z, gain.shape[1]
    return pl.pallas_call(
        functools.partial(gather_kernel, count_z),
        out_shape=[jax.ShapeDtypeStruct((rows, width), BF16)] * count_z,
        in_specs=[VMEM] * (1 + len(parts)),
        out_specs=[VMEM] * count_z,
        compiler_params=pltpu.CompilerParams(vmem_limit_bytes=8 * MIB),
        cost_estimate=cost(8 * len(parts) * rows * count_z * width, 4 * rows * count_z * width),
        name="gather_slots",
    )(gain, *parts)


def expert_kernel(count_z, slots_exp, core_ref, _, in_own, out_own, in_other, out_other, *refs):
    parts, outs = refs[:count_z], refs[count_z : 2 * count_z]
    rows_ref, sum_ref, in_ref, out_ref, sems = refs[2 * count_z :]
    each = parts[0].shape[0]
    per_core = in_own.shape[0]
    copies = []
    for which, pair in enumerate(((in_own, out_own), (in_other, out_other))):
        for at in range(per_core):
            place = which * per_core + at
            for kind, (source, target) in enumerate(zip(pair, (in_ref, out_ref))):
                copies.append(
                    pltpu.make_async_copy(
                        source.at[at], target.at[place], sems.at[2 * place + kind]
                    )
                )
                copies[-1].start()
    for at, ref in enumerate(parts):
        rows_ref[at * each : (at + 1) * each, :] = ref[...]
    rows = rows_ref[...]
    place = lax.broadcasted_iota(jnp.int32, (rows.shape[0], 1), 0)
    expert = lax.rem(place, each) // slots_exp
    core = core_ref[0]

    for at in range(2 * per_core):
        held = core if at < per_core else 1 - core
        mine = expert == held * per_core + at % per_core
        copies[2 * at].wait()
        hidden = jax.nn.gelu(jnp.dot(rows, in_ref[at], preferred_element_type=F32))
        hidden = jnp.where(mine, hidden, 0.0).astype(BF16)
        copies[2 * at + 1].wait()
        made = jnp.dot(hidden, out_ref[at], preferred_element_type=F32)
        if at == 0:
            sum_ref[...] = made
        else:
            sum_ref[...] += made
    for at, out in enumerate(outs):
        out[...] = sum_ref[at * each : (at + 1) * each, :].astype(BF16)


def experts(core, after, parts, w_in, w_out, in_other, out_other, slots_exp):
    count_z = len(parts)
    each, width = parts[0].shape
    per_core, _, inner = w_in.shape
    rows = each * count_z
    return pl.pallas_call(
        functools.partial(expert_kernel, count_z, slots_exp),
        out_shape=[jax.ShapeDtypeStruct((each, width), BF16)] * count_z,
        in_specs=[SMEM, ANY, HBM, HBM, HBM, HBM] + [VMEM] * count_z,
        out_specs=[VMEM] * count_z,
        scratch_shapes=[
            pltpu.VMEM((rows, width), BF16),
            pltpu.VMEM((rows, width), F32),
            pltpu.VMEM((2 * per_core, width, inner), BF16),
            pltpu.VMEM((2 * per_core, inner, width), BF16),
            pltpu.SemaphoreType.DMA((4 * per_core,)),
        ],
        compiler_params=pltpu.CompilerParams(vmem_limit_bytes=LIMIT_E * MIB),
        cost_estimate=cost(8 * rows * width * inner * per_core, 8 * width * inner * per_core),
        name="experts",
    )(core, after, w_in, w_out, in_other, out_other, *parts)


def copy_kernel(start_ref, cells_ref, _, out_ref):
    rows = out_ref.shape[0]
    out_ref[...] = cells_ref[pl.ds(pl.multiple_of(start_ref[0], LANES), rows), :]


def edge_rows(start, cells, rows, after):
    return pl.pallas_call(
        copy_kernel,
        out_shape=jax.ShapeDtypeStruct((rows, cells.shape[1]), BF16),
        in_specs=[SMEM, VMEM, ANY],
        out_specs=VMEM,
        compiler_params=pltpu.CompilerParams(vmem_limit_bytes=8 * MIB),
        cost_estimate=cost(0, 4 * rows * cells.shape[1]),
        name="edge_rows",
    )(start, cells, after)


def combine_kernel(count, valid_ref, keys_ref, gain_ref, _, *refs):
    block = 128
    if len(refs) > 2 * count:
        fill_spectrum(refs[count], refs[count + 1], refs[-1])
        refs = refs[:count] + refs[count + 2 : -1]
    for at, (cells_ref, out_ref) in enumerate(zip(refs[:count], refs[count:])):
        for start in range(0, cells_ref.shape[0], block):
            rows = slice(start, start + block)
            normed = rms_scale(cells_ref[rows, :].astype(F32), gain_ref[...]).astype(BF16)
            logits = dot_nt(normed, keys_ref[...])
            raised = jnp.exp(logits - jnp.max(logits, axis=-1, keepdims=True))
            share = raised * (1.0 / jnp.sum(raised, axis=-1, keepdims=True))
            out_ref[rows, :] = jnp.where(valid_ref[at] > 0, share, 0.0).astype(BF16)


def combine_weights(valid, cells, keys, gain, after, filters=()):
    made = [(filters[1].shape[0], filters[0].shape[0], filters[1].shape[2])] if filters else []
    width, slots = gain.shape[1], keys.shape[0]
    total = sum(part.shape[0] for part in cells)
    return pl.pallas_call(
        functools.partial(combine_kernel, len(cells)),
        out_shape=[jax.ShapeDtypeStruct((part.shape[0], slots), BF16) for part in cells]
        + [jax.ShapeDtypeStruct(shape, F32) for shape in made],
        in_specs=[SMEM, VMEM, VMEM, ANY] + [VMEM] * (len(cells) + len(filters)),
        out_specs=[VMEM] * (len(cells) + len(made)),
        compiler_params=pltpu.CompilerParams(vmem_limit_bytes=16 * MIB),
        cost_estimate=cost(2 * total * width * slots, 2 * total * width, total * slots),
        name="combine_weights",
    )(valid, keys, gain, after, *cells, *filters)


def batch(rows):
    return next(count for count in (8, 4, 2, 1) if rows % count == 0)


def pieces(value, count):
    out = []
    for _ in range(count):
        piece = value.astype(BF16)
        out.append(piece)
        value = value - piece.astype(value.dtype)
    return out


def wave(cols, taps):
    half = cols // 2
    freq = np.arange(half)[:, None]
    angle = 2 * np.pi * ((freq * np.arange(cols)[None, :]) % cols) / cols
    sign = np.where(np.arange(cols) % 2 == 0, 1.0, -1.0)
    real, imag = np.cos(angle), -np.sin(angle)
    imag[0] = sign
    to_freq = np.concatenate([real, imag], axis=0)
    back_real, back_imag = 2 * np.cos(angle).T / cols, -2 * np.sin(angle).T / cols
    back_real[:, 0] = sign / cols
    back_imag[:, 0] = 1 / cols
    to_cols = np.concatenate([back_real, back_imag], axis=1)
    offset = np.arange(taps) - taps // 2
    turn = 2 * np.pi * freq * offset[None, :] / cols
    first, second, third = np.cos(turn), np.sin(turn) - np.cos(turn), np.sin(turn) + np.cos(turn)
    first[0], second[0] = 0.0, 1.0
    third[0] = np.where(offset % 2 == 0, -1.0, 1.0)
    spectrum = np.zeros((3 * half, 8))
    spectrum[:, :taps] = np.concatenate([first, second, third], axis=0)

    def split(value):
        high = value.astype(np.float32).astype(ml_dtypes.bfloat16)
        return high, (value - high.astype(np.float64)).astype(np.float32).astype(ml_dtypes.bfloat16)

    f_high, f_low = split(to_freq)
    c_high, c_low = split(to_cols)
    s_high, s_low = split(spectrum)
    return (
        np.concatenate([f_high, f_low], axis=1),
        np.concatenate([c_high, c_high], axis=1),
        c_low,
        np.concatenate([s_high, s_high, s_high, s_low, s_low], axis=1),
    )


def fill_spectrum(coef_ref, weight_ref, out_ref):
    taps, _, width = weight_ref.shape
    fill = jnp.zeros((8 - taps, width), F32)
    for tap in range(taps):
        row = jnp.concatenate([weight_ref[tap], fill], axis=0)
        one, two, three = (p.astype(F32) for p in pieces(row, 3))
        stack = jnp.concatenate([one, two, three, one, two], axis=0).astype(BF16)
        out_ref[tap] = jnp.dot(coef_ref[...], stack, preferred_element_type=F32)


def block_kernel(
    dims, place_ref, cells_ref, low_ref, high_ref, share_ref, share_low, share_high, spectrum_ref, freq_ref,
    cols_ref, fine_ref, ln_ref, proj_ref, scale_ref, *rest
):
    rows, cols, taps = dims
    slot_refs, out_ref = rest[:-6], rest[-6]
    slots_ref, state_ref, freqs_ref, back_ref, conv_ref = rest[-5:]
    reach = taps // 2
    half = cols // 2
    width = cells_ref.shape[1]
    start = 0
    for ref in slot_refs:
        slots_ref[start : start + ref.shape[0], :] = ref[...]
        start += ref.shape[0]
    chunk = 2 * LANES

    def mix(cells, share, row, to, keep):
        at = pl.ds(pl.multiple_of(row * cols, cols), cols)
        picked = share[at, :]
        for lane in range(0, width, chunk):
            lanes = slice(lane, lane + chunk)
            mixed = jnp.dot(picked, slots_ref[:, lanes], preferred_element_type=F32)
            state = (cells[at, lanes].astype(F32) + mixed).astype(BF16)
            if keep:
                state_ref[at, lanes] = state
            twice = jnp.concatenate([state, state], axis=0)
            freqs_ref[to, :, lanes] = jnp.dot(freq_ref[...], twice, preferred_element_type=F32)

    for row in range(reach):
        mix(low_ref, share_low, row, row + place_ref[0], False)
        mix(high_ref, share_high, row, row + place_ref[1], False)

    at_once = batch(rows)

    @pl.loop(0, rows // at_once)
    def _(step):
        for extra in range(at_once):
            row = step * at_once + extra
            mix(cells_ref, share_ref, row, row + reach, True)

    tile = 16

    @pl.loop(0, width // LANES)
    def _(group):
        lanes = pl.ds(pl.multiple_of(group * LANES, LANES), LANES)

        @pl.loop(0, half // tile)
        def _(step):
            base = pl.multiple_of(step * tile, tile)
            for first in range(0, rows, 8):
                parts = ([], [])
                for sub in range(0, tile, 8):
                    real_at, imag_at = pl.ds(base + sub, 8), pl.ds(base + half + sub, 8)
                    third_at = pl.ds(base + 2 * half + sub, 8)
                    weights = [
                        [spectrum_ref[tap, at, lanes] for tap in range(taps)]
                        for at in (real_at, imag_at, third_at)
                    ]
                    sums = [[None] * 8 for _ in range(3)]
                    for row in range(8 + taps - 1):
                        real = freqs_ref[first + row, real_at, lanes]
                        imag = freqs_ref[first + row, imag_at, lanes]
                        for kind, value in enumerate((real + imag, real, imag)):
                            for to in range(max(0, row - taps + 1), min(8, row + 1)):
                                term = value * weights[kind][row - to]
                                have = sums[kind][to]
                                sums[kind][to] = term if have is None else have + term
                    parts[0].append([sums[0][to] - sums[2][to] for to in range(8)])
                    parts[1].append([sums[0][to] + sums[1][to] for to in range(8)])
                for to in range(8):
                    for which in range(2):
                        value = jnp.concatenate([sub[to] for sub in parts[which]], axis=0)
                        high, low = pieces(value, 2)
                        back_ref[first + to, pl.ds(base + which * half, tile), lanes] = high
                        back_ref[first + to, pl.ds(base + cols + which * half, tile), lanes] = low

    pair = batch(rows)

    @pl.loop(0, rows // pair)
    def _(step):
        for one in range(pair):
            total = None
            for lane in range(0, width, chunk):
                lanes = slice(lane, lane + chunk)
                row = step * pair + one
                conv = jnp.dot(cols_ref[...], back_ref[row, :, lanes], preferred_element_type=F32)
                conv += jnp.dot(fine_ref[...], back_ref[row, :cols, lanes], preferred_element_type=F32)
                conv_ref[one * cols : (one + 1) * cols, lanes] = conv
        at = pl.ds(pl.multiple_of(step * (pair * cols), pair * cols), pair * cols)
        conv = conv_ref[...]
        center = conv - jnp.mean(conv, axis=-1, keepdims=True)
        spread = jnp.mean(center * center, axis=-1, keepdims=True)
        normal = (center * lax.rsqrt(spread + EPS) * ln_ref[...]).astype(BF16)
        for lane in range(0, width, chunk):
            lanes = slice(lane, lane + chunk)
            branch = jnp.dot(normal, proj_ref[:, lanes], preferred_element_type=F32)
            branch = scale_ref[:, lanes] * jax.nn.gelu(branch)
            out_ref[at, lanes] = (state_ref[at, lanes].astype(F32) + branch).astype(BF16)


def block_fields(dims, places, cells, halo, shares, weight, ln_gain, proj, scale, slot_parts, waves):
    rows, cols, taps = dims
    total, width = cells.shape
    slots = sum(part.shape[0] for part in slot_parts)
    padded = rows + taps - 1
    return pl.pallas_call(
        functools.partial(block_kernel, dims),
        out_shape=jax.ShapeDtypeStruct((total, width), BF16),
        in_specs=[SMEM] + [VMEM] * (13 + len(slot_parts)),
        out_specs=VMEM,
        scratch_shapes=[
            pltpu.VMEM((slots, width), BF16),
            pltpu.VMEM((total, width), BF16),
            pltpu.VMEM((padded, cols, width), F32),
            pltpu.VMEM((rows, 2 * cols, width), BF16),
            pltpu.VMEM((batch(rows) * cols, width), F32),
        ],
        compiler_params=pltpu.CompilerParams(vmem_limit_bytes=32 * MIB),
        cost_estimate=cost(6 * total * width * width, 8 * total * width, total * width),
        name="block_fields",
    )(places, cells, *halo, *shares, weight, *waves, ln_gain, proj, scale, *slot_parts)


def local(
    tokens, slot_keys, norm_gain, slot_gain, w_in, w_out, conv_weight, ln_gain, proj, layer_scale
):
    rows, cols, width = tokens.shape[1:]
    count_fc = lax.axis_size("fc")
    count_tok = lax.axis_size("tok")
    count_z = count_fc // 2
    slots = slot_keys.shape[1]
    slot_dev = slots // (count_fc * count_tok)
    slots_exp = slot_dev // w_in.shape[0]
    taps = conv_weight.shape[0]
    reach = taps // 2
    at_fc, at_tok = lax.axis_index("fc"), lax.axis_index("tok")
    other = [(i, i ^ 1) for i in range(count_fc)]
    cells = tokens.reshape(rows * cols, width)
    norm_gain, slot_gain = norm_gain.reshape(1, width), slot_gain.reshape(1, width)
    ln_gain, layer_scale = ln_gain.reshape(1, width), layer_scale.reshape(1, width)

    def shift(value, axis, step):
        count = lax.axis_size(axis)
        return lax.ppermute(value, axis, [(i, (i + step) % count) for i in range(count)])

    other = [(i, i ^ 1) for i in range(count_fc)]
    tie = lax.optimization_barrier
    even = at_tok % 2 == 0
    last = (rows - reach) * cols

    def swap(start):
        pairs = [(i, i + 1) for i in range(start, count_tok - 1, 2)]
        return pairs + [(j, i) for i, j in pairs]

    edge = lax.dynamic_slice_in_dim(cells, jnp.where(even, last, 0), reach * cols, axis=0)
    first_halo = lax.ppermute(edge, "tok", swap(0))
    in_other = lax.ppermute(w_in, "fc", other)
    out_other = lax.ppermute(w_out, "fc", other)

    index = jnp.stack([at_fc // 2, at_tok]).astype(jnp.int32)
    keys, *numer = dispatch(index, cells, slot_keys, norm_gain, (count_z, count_tok, slot_dev))
    numer[1], in_other, out_other = tie((numer[1], in_other, out_other))
    parts = [numer[0]] + [shift(numer[k], "tok", k) for k in range(1, count_tok)]

    slot_in = gather_slots(parts, slot_gain, count_z)
    arrived = [slot_in[0]] + [shift(slot_in[k], "fc", 2 * k) for k in range(1, count_z)]
    first = edge_rows(jnp.where(even, 0, last).reshape(1), cells, reach * cols, slot_in[0])
    second_halo = lax.ppermute(first, "tok", swap(1))
    always = jnp.ones((1,), jnp.int32)
    (share,) = combine_weights(always, [cells], keys, norm_gain, first)
    core = (at_fc % 2).astype(jnp.int32).reshape(1)
    made = experts(core, share, arrived, w_in, w_out, in_other, out_other, slots_exp)
    back = [made[0]] + [shift(made[k], "fc", -2 * k) for k in range(1, count_z)]
    mine = jnp.concatenate(back, axis=0)
    above, below = at_tok > 0, at_tok < count_tok - 1
    inside = jnp.stack([jnp.where(even, below, above), jnp.where(even, above, below)])
    halo = (first_halo, second_halo)
    freq, to_cols, fine, coef = wave(cols, taps)
    *halo_shares, filters = combine_weights(
        inside.astype(jnp.int32), halo, keys, norm_gain, made[0], (coef, conv_weight)
    )
    places = jnp.where(even, jnp.array([rows + reach, 0]), jnp.array([0, rows + reach]))
    every = [mine] + [shift(mine, "tok", -k) for k in range(1, count_tok)]

    fields = block_fields(
        (rows, cols, taps), places.astype(jnp.int32), cells, halo, (share, *halo_shares), filters,
        ln_gain, proj, layer_scale, every, (freq, to_cols, fine),
    )
    return fields.reshape(1, rows, cols, width)


def solution(mesh):
    return jax.shard_map(
        local,
        mesh=mesh,
        in_specs=(
            P("fc", "tok", None, None),
            P(),
            P(),
            P(),
            P(("fc", "tok"), None, None),
            P(("fc", "tok"), None, None),
            P(),
            P(),
            P(),
            P(),
        ),
        out_specs=P("fc", "tok", None, None),
        check_vma=False,
    )
```

```python
import functools

import jax
import jax.numpy as jnp
import ml_dtypes
import numpy as np
from jax import lax
from jax.experimental import pallas as pl
from jax.experimental.pallas import tpu as pltpu
from jax.sharding import PartitionSpec as P

F32 = jnp.float32
BF16 = jnp.bfloat16
LANES = 128
EPS = 1e-06
MIB = 1024 * 1024
LIMIT_D = 56
LIMIT_E = 16
NT = (((1,), (1,)), ((), ()))
VMEM = pl.BlockSpec(memory_space=pltpu.VMEM)
SMEM = pl.BlockSpec(memory_space=pltpu.SMEM)
HBM = pl.BlockSpec(memory_space=pltpu.HBM)
ANY = pl.BlockSpec(memory_space=pl.ANY)


def dot_nt(left, right):
    return lax.dot_general(left, right, NT, preferred_element_type=F32)


def rms_scale(value, gain):
    return value * lax.rsqrt(jnp.mean(value * value, axis=-1, keepdims=True) + EPS) * gain


def split_index(value, count):
    if count & (count - 1) == 0:
        return value >> (count.bit_length() - 1), value & (count - 1)
    return value // count, lax.rem(value, count)


def cost(flops, moved, exps=0):
    return pl.CostEstimate(flops=flops, bytes_accessed=moved, transcendentals=exps)


def dispatch_kernel(layout, index_ref, cells_hbm, keys_hbm, gain_ref, keys_out, *rest):
    count_z, count_tok, slot_dev = layout
    outs, (cells_ref, keys_ref, normed_ref, cell_sems, key_sem) = rest[:-5], rest[-5:]
    total, width = cells_ref.shape
    slots = keys_ref.shape[1]
    my_z, my_tok = index_ref[0], index_ref[1]
    count = cell_sems.shape[0]
    block = total // count
    key_copy = pltpu.make_async_copy(keys_hbm, keys_ref, key_sem)
    key_copy.start()
    copies = []
    for step in range(count):
        rows = slice(step * block, (step + 1) * block)
        copies.append(
            pltpu.make_async_copy(cells_hbm.at[rows], cells_ref.at[rows], cell_sems.at[step])
        )
        copies[-1].start()
    place = lax.broadcasted_iota(jnp.int32, (slots, 1), 0)
    source = lax.broadcasted_iota(jnp.int32, (slots, slots), 1)
    outer, inner = split_index(place, slot_dev)
    outer, core = split_index(outer, 2)
    step_tok, step_z = split_index(outer, count_z)
    at_z = split_index(step_z + my_z, count_z)[1]
    at_tok = split_index(step_tok + my_tok, count_tok)[1]
    wanted = ((at_z * 2 + core) * count_tok + at_tok) * slot_dev + inner
    pick = jnp.where(wanted == source, 1.0, 0.0).astype(BF16)
    key_copy.wait()
    keys = dot_nt(pick, keys_ref[...]).astype(BF16)
    keys_out[...] = keys

    for step in range(count):
        rows = slice(step * block, (step + 1) * block)
        copies[step].wait()
        normed_ref[rows, :] = rms_scale(cells_ref[rows, :].astype(F32), gain_ref[...]).astype(BF16)

    part = slots // count_tok
    logits = dot_nt(keys, normed_ref[...])
    peak = jnp.max(logits, axis=1, keepdims=True)
    weight = jnp.exp(logits - peak).astype(BF16)
    first = peak.astype(BF16).astype(F32)
    second = (peak - first).astype(BF16).astype(F32)
    third = peak - first - second
    lane = lax.broadcasted_iota(jnp.int32, (slots, LANES), 1)
    marks = jnp.where(
        lane == 0, first, jnp.where(lane == 1, second, jnp.where(lane == 2, third, 0.0))
    ).astype(BF16)
    for at, out in enumerate(outs):
        out[:, width:] = marks[at * part : (at + 1) * part, :]
    for lane in range(0, width, 2 * LANES):
        lanes = slice(lane, lane + 2 * LANES)
        numer = jnp.dot(weight, cells_ref[:, lanes], preferred_element_type=F32).astype(BF16)
        for at, out in enumerate(outs):
            out[:, lanes] = numer[at * part : (at + 1) * part, :]


def dispatch(index, cells, keys, gain, layout):
    count_z, count_tok, slot_dev = layout
    total, width = cells.shape
    slots = keys.shape[1]
    part = slots // count_tok
    count = 8
    return pl.pallas_call(
        functools.partial(dispatch_kernel, layout),
        out_shape=[jax.ShapeDtypeStruct((slots, width), BF16)]
        + [jax.ShapeDtypeStruct((part, width + LANES), BF16)] * count_tok,
        in_specs=[SMEM, HBM, HBM, VMEM],
        out_specs=[VMEM] * (1 + count_tok),
        scratch_shapes=[
            pltpu.VMEM((total, width), BF16),
            pltpu.VMEM((width, slots), BF16),
            pltpu.VMEM((total, width), BF16),
            pltpu.SemaphoreType.DMA((count,)),
            pltpu.SemaphoreType.DMA,
        ],
        compiler_params=pltpu.CompilerParams(vmem_limit_bytes=LIMIT_D * MIB),
        cost_estimate=cost(4 * total * width * slots, 4 * total * width, total * slots),
        name="dispatch",
    )(index, cells, keys, gain)


def gather_kernel(count_z, gain_ref, *refs):
    count = len(refs) - count_z
    parts, outs = refs[:count], refs[count:]
    width = gain_ref.shape[1]
    peaks = []
    for ref in parts:
        piece = ref[:, width:].astype(F32)
        peaks.append(jnp.sum(piece, axis=1, keepdims=True))
    peak = functools.reduce(jnp.maximum, peaks)
    numer = None
    for ref, own in zip(parts, peaks):
        term = ref[:, :width].astype(F32) * jnp.exp(own - peak)
        numer = term if numer is None else numer + term
    value = rms_scale(numer, gain_ref[...]).astype(BF16)
    rows = value.shape[0] // count_z
    for at, out in enumerate(outs):
        out[...] = value[at * rows : (at + 1) * rows, :]


def gather_slots(parts, gain, count_z):
    rows, width = parts[0].shape[0] // count_z, gain.shape[1]
    return pl.pallas_call(
        functools.partial(gather_kernel, count_z),
        out_shape=[jax.ShapeDtypeStruct((rows, width), BF16)] * count_z,
        in_specs=[VMEM] * (1 + len(parts)),
        out_specs=[VMEM] * count_z,
        compiler_params=pltpu.CompilerParams(vmem_limit_bytes=8 * MIB),
        cost_estimate=cost(8 * len(parts) * rows * count_z * width, 4 * rows * count_z * width),
        name="gather_slots",
    )(gain, *parts)


def expert_kernel(count_z, slots_exp, core_ref, _, in_own, out_own, in_other, out_other, *refs):
    parts, outs = refs[:count_z], refs[count_z : 2 * count_z]
    rows_ref, sum_ref, in_ref, out_ref, sems = refs[2 * count_z :]
    each = parts[0].shape[0]
    per_core = in_own.shape[0]
    copies = []
    for which, pair in enumerate(((in_own, out_own), (in_other, out_other))):
        for at in range(per_core):
            place = which * per_core + at
            for kind, (source, target) in enumerate(zip(pair, (in_ref, out_ref))):
                copies.append(
                    pltpu.make_async_copy(
                        source.at[at], target.at[place], sems.at[2 * place + kind]
                    )
                )
                copies[-1].start()
    for at, ref in enumerate(parts):
        rows_ref[at * each : (at + 1) * each, :] = ref[...]
    rows = rows_ref[...]
    place = lax.broadcasted_iota(jnp.int32, (rows.shape[0], 1), 0)
    expert = lax.rem(place, each) // slots_exp
    core = core_ref[0]

    for at in range(2 * per_core):
        held = core if at < per_core else 1 - core
        mine = expert == held * per_core + at % per_core
        copies[2 * at].wait()
        hidden = jax.nn.gelu(jnp.dot(rows, in_ref[at], preferred_element_type=F32))
        hidden = jnp.where(mine, hidden, 0.0).astype(BF16)
        copies[2 * at + 1].wait()
        made = jnp.dot(hidden, out_ref[at], preferred_element_type=F32)
        if at == 0:
            sum_ref[...] = made
        else:
            sum_ref[...] += made
    for at, out in enumerate(outs):
        out[...] = sum_ref[at * each : (at + 1) * each, :].astype(BF16)


def experts(core, after, parts, w_in, w_out, in_other, out_other, slots_exp):
    count_z = len(parts)
    each, width = parts[0].shape
    per_core, _, inner = w_in.shape
    rows = each * count_z
    return pl.pallas_call(
        functools.partial(expert_kernel, count_z, slots_exp),
        out_shape=[jax.ShapeDtypeStruct((each, width), BF16)] * count_z,
        in_specs=[SMEM, ANY, HBM, HBM, HBM, HBM] + [VMEM] * count_z,
        out_specs=[VMEM] * count_z,
        scratch_shapes=[
            pltpu.VMEM((rows, width), BF16),
            pltpu.VMEM((rows, width), F32),
            pltpu.VMEM((2 * per_core, width, inner), BF16),
            pltpu.VMEM((2 * per_core, inner, width), BF16),
            pltpu.SemaphoreType.DMA((4 * per_core,)),
        ],
        compiler_params=pltpu.CompilerParams(vmem_limit_bytes=LIMIT_E * MIB),
        cost_estimate=cost(8 * rows * width * inner * per_core, 8 * width * inner * per_core),
        name="experts",
    )(core, after, w_in, w_out, in_other, out_other, *parts)


def pass_kernel(value_ref, _, out_ref):
    out_ref[...] = value_ref[...]


def after(value, other):
    return pl.pallas_call(
        pass_kernel,
        out_shape=jax.ShapeDtypeStruct(value.shape, value.dtype),
        in_specs=[VMEM, ANY],
        out_specs=VMEM,
        compiler_params=pltpu.CompilerParams(vmem_limit_bytes=8 * MIB),
        cost_estimate=cost(0, 4 * value.size),
        name="after",
    )(value, other)


def copy_kernel(lane, start_ref, cells_ref, _, out_ref):
    rows, wide = out_ref.shape
    at = pl.ds(pl.multiple_of(start_ref[0], LANES), rows)
    out_ref[...] = cells_ref[at, lane : lane + wide]


def edge_rows(start, cells, rows, lane, wide, after):
    return pl.pallas_call(
        functools.partial(copy_kernel, lane),
        out_shape=jax.ShapeDtypeStruct((rows, wide), BF16),
        in_specs=[SMEM, VMEM, ANY],
        out_specs=VMEM,
        compiler_params=pltpu.CompilerParams(vmem_limit_bytes=8 * MIB),
        cost_estimate=cost(0, 4 * rows * cells.shape[1]),
        name="edge_rows",
    )(start, cells, after)


def combine_kernel(counts, valid_ref, keys_ref, gain_ref, _, *refs):
    block = 128
    total = sum(counts)
    sources, refs = refs[:total], refs[total:]
    if len(refs) > len(counts):
        fill_spectrum(refs[0], refs[1], refs[-1])
        refs = refs[2:-1]
    for at, (count, out_ref) in enumerate(zip(counts, refs)):
        held, sources = sources[:count], sources[count:]
        for start in range(0, out_ref.shape[0], block):
            rows = slice(start, start + block)
            cells = jnp.concatenate([ref[rows, :] for ref in held], axis=1).astype(F32)
            normed = rms_scale(cells, gain_ref[...]).astype(BF16)
            logits = dot_nt(normed, keys_ref[...])
            raised = jnp.exp(logits - jnp.max(logits, axis=-1, keepdims=True))
            share = raised * (1.0 / jnp.sum(raised, axis=-1, keepdims=True))
            out_ref[rows, :] = jnp.where(valid_ref[at] > 0, share, 0.0).astype(BF16)


def combine_weights(valid, cells, keys, gain, after, filters=()):
    made = [(filters[1].shape[0], filters[0].shape[0], filters[1].shape[2])] if filters else []
    width, slots = gain.shape[1], keys.shape[0]
    total = sum(parts[0].shape[0] for parts in cells)
    flat = [part for parts in cells for part in parts]
    return pl.pallas_call(
        functools.partial(combine_kernel, [len(parts) for parts in cells]),
        out_shape=[jax.ShapeDtypeStruct((parts[0].shape[0], slots), BF16) for parts in cells]
        + [jax.ShapeDtypeStruct(shape, F32) for shape in made],
        in_specs=[SMEM, VMEM, VMEM, ANY] + [VMEM] * (len(flat) + len(filters)),
        out_specs=[VMEM] * (len(cells) + len(made)),
        compiler_params=pltpu.CompilerParams(vmem_limit_bytes=16 * MIB),
        cost_estimate=cost(2 * total * width * slots, 2 * total * width, total * slots),
        name="combine_weights",
    )(valid, keys, gain, after, *flat, *filters)


def batch(rows):
    return next(count for count in (8, 4, 2, 1) if rows % count == 0)


def pieces(value, count):
    out = []
    for _ in range(count):
        piece = value.astype(BF16)
        out.append(piece)
        value = value - piece.astype(value.dtype)
    return out


def wave(cols, taps):
    half = cols // 2
    freq = np.arange(half)[:, None]
    angle = 2 * np.pi * ((freq * np.arange(cols)[None, :]) % cols) / cols
    sign = np.where(np.arange(cols) % 2 == 0, 1.0, -1.0)
    real, imag = np.cos(angle), -np.sin(angle)
    imag[0] = sign
    to_freq = np.concatenate([real, imag], axis=0)
    back_real, back_imag = 2 * np.cos(angle).T / cols, -2 * np.sin(angle).T / cols
    back_real[:, 0] = sign / cols
    back_imag[:, 0] = 1 / cols
    to_cols = np.concatenate([back_real, back_imag], axis=1)
    offset = np.arange(taps) - taps // 2
    turn = 2 * np.pi * freq * offset[None, :] / cols
    first, second, third = np.cos(turn), np.sin(turn) - np.cos(turn), np.sin(turn) + np.cos(turn)
    first[0], second[0] = 0.0, 1.0
    third[0] = np.where(offset % 2 == 0, -1.0, 1.0)
    spectrum = np.zeros((3 * half, 8))
    spectrum[:, :taps] = np.concatenate([first, second, third], axis=0)

    def split(value):
        high = value.astype(np.float32).astype(ml_dtypes.bfloat16)
        return high, (value - high.astype(np.float64)).astype(np.float32).astype(ml_dtypes.bfloat16)

    f_high, f_low = split(to_freq)
    c_high, c_low = split(to_cols)
    s_high, s_low = split(spectrum)
    return (
        np.concatenate([f_high, f_low], axis=1),
        np.concatenate([c_high, c_high], axis=1),
        c_low,
        np.concatenate([s_high, s_high, s_high, s_low, s_low], axis=1),
    )


def fill_spectrum(coef_ref, weight_ref, out_ref):
    taps, _, width = weight_ref.shape
    fill = jnp.zeros((8 - taps, width), F32)
    for tap in range(taps):
        row = jnp.concatenate([weight_ref[tap], fill], axis=0)
        one, two, three = (p.astype(F32) for p in pieces(row, 3))
        stack = jnp.concatenate([one, two, three, one, two], axis=0).astype(BF16)
        out_ref[tap] = jnp.dot(coef_ref[...], stack, preferred_element_type=F32)


def block_kernel(
    dims, place_ref, cells_ref, first_ref, second_a, second_b, share_ref, share_low, share_high, spectrum_ref, freq_ref,
    cols_ref, fine_ref, ln_ref, proj_ref, scale_ref, *rest
):
    rows, cols, taps = dims
    slot_refs, out_ref = rest[:-6], rest[-6]
    slots_ref, state_ref, freqs_ref, back_ref, conv_ref = rest[-5:]
    reach = taps // 2
    half = cols // 2
    width = cells_ref.shape[1]
    start = 0
    for ref in slot_refs:
        slots_ref[start : start + ref.shape[0], :] = ref[...]
        start += ref.shape[0]
    chunk = 2 * LANES

    def mix(cells, share, row, to, keep):
        at = pl.ds(pl.multiple_of(row * cols, cols), cols)
        picked = share[at, :]
        for lane in range(0, width, chunk):
            lanes = slice(lane, lane + chunk)
            mixed = jnp.dot(picked, slots_ref[:, lanes], preferred_element_type=F32)
            wide = cells[0].shape[1]
            held = cells[lane // wide][at, lane % wide : lane % wide + chunk]
            state = (held.astype(F32) + mixed).astype(BF16)
            if keep:
                state_ref[at, lanes] = state
            twice = jnp.concatenate([state, state], axis=0)
            freqs_ref[to, :, lanes] = jnp.dot(freq_ref[...], twice, preferred_element_type=F32)

    for row in range(reach):
        mix((first_ref,), share_low, row, row + place_ref[0], False)
        mix((second_a, second_b), share_high, row, row + place_ref[1], False)

    at_once = batch(rows)

    @pl.loop(0, rows // at_once)
    def _(step):
        for extra in range(at_once):
            row = step * at_once + extra
            mix((cells_ref,), share_ref, row, row + reach, True)

    tile = 16

    @pl.loop(0, width // LANES)
    def _(group):
        lanes = pl.ds(pl.multiple_of(group * LANES, LANES), LANES)

        @pl.loop(0, half // tile)
        def _(step):
            base = pl.multiple_of(step * tile, tile)
            for first in range(0, rows, 8):
                parts = ([], [])
                for sub in range(0, tile, 8):
                    real_at, imag_at = pl.ds(base + sub, 8), pl.ds(base + half + sub, 8)
                    third_at = pl.ds(base + 2 * half + sub, 8)
                    weights = [
                        [spectrum_ref[tap, at, lanes] for tap in range(taps)]
                        for at in (real_at, imag_at, third_at)
                    ]
                    sums = [[None] * 8 for _ in range(3)]
                    for row in range(8 + taps - 1):
                        real = freqs_ref[first + row, real_at, lanes]
                        imag = freqs_ref[first + row, imag_at, lanes]
                        for kind, value in enumerate((real + imag, real, imag)):
                            for to in range(max(0, row - taps + 1), min(8, row + 1)):
                                term = value * weights[kind][row - to]
                                have = sums[kind][to]
                                sums[kind][to] = term if have is None else have + term
                    parts[0].append([sums[0][to] - sums[2][to] for to in range(8)])
                    parts[1].append([sums[0][to] + sums[1][to] for to in range(8)])
                for to in range(8):
                    for which in range(2):
                        value = jnp.concatenate([sub[to] for sub in parts[which]], axis=0)
                        high, low = pieces(value, 2)
                        back_ref[first + to, pl.ds(base + which * half, tile), lanes] = high
                        back_ref[first + to, pl.ds(base + cols + which * half, tile), lanes] = low

    pair = batch(rows)

    @pl.loop(0, rows // pair)
    def _(step):
        for one in range(pair):
            total = None
            for lane in range(0, width, chunk):
                lanes = slice(lane, lane + chunk)
                row = step * pair + one
                conv = jnp.dot(cols_ref[...], back_ref[row, :, lanes], preferred_element_type=F32)
                conv += jnp.dot(fine_ref[...], back_ref[row, :cols, lanes], preferred_element_type=F32)
                conv_ref[one * cols : (one + 1) * cols, lanes] = conv
        at = pl.ds(pl.multiple_of(step * (pair * cols), pair * cols), pair * cols)
        conv = conv_ref[...]
        center = conv - jnp.mean(conv, axis=-1, keepdims=True)
        spread = jnp.mean(center * center, axis=-1, keepdims=True)
        normal = (center * lax.rsqrt(spread + EPS) * ln_ref[...]).astype(BF16)
        for lane in range(0, width, chunk):
            lanes = slice(lane, lane + chunk)
            branch = jnp.dot(normal, proj_ref[:, lanes], preferred_element_type=F32)
            branch = scale_ref[:, lanes] * jax.nn.gelu(branch)
            out_ref[at, lanes] = (state_ref[at, lanes].astype(F32) + branch).astype(BF16)


def block_fields(dims, places, cells, halo, shares, weight, ln_gain, proj, scale, slot_parts, waves):
    rows, cols, taps = dims
    total, width = cells.shape
    slots = sum(part.shape[0] for part in slot_parts)
    padded = rows + taps - 1
    return pl.pallas_call(
        functools.partial(block_kernel, dims),
        out_shape=jax.ShapeDtypeStruct((total, width), BF16),
        in_specs=[SMEM] + [VMEM] * (14 + len(slot_parts)),
        out_specs=VMEM,
        scratch_shapes=[
            pltpu.VMEM((slots, width), BF16),
            pltpu.VMEM((total, width), BF16),
            pltpu.VMEM((padded, cols, width), F32),
            pltpu.VMEM((rows, 2 * cols, width), BF16),
            pltpu.VMEM((batch(rows) * cols, width), F32),
        ],
        compiler_params=pltpu.CompilerParams(vmem_limit_bytes=32 * MIB),
        cost_estimate=cost(6 * total * width * width, 8 * total * width, total * width),
        name="block_fields",
    )(places, cells, *halo, *shares, weight, *waves, ln_gain, proj, scale, *slot_parts)


def local(
    tokens, slot_keys, norm_gain, slot_gain, w_in, w_out, conv_weight, ln_gain, proj, layer_scale
):
    rows, cols, width = tokens.shape[1:]
    count_fc = lax.axis_size("fc")
    count_tok = lax.axis_size("tok")
    count_z = count_fc // 2
    slots = slot_keys.shape[1]
    slot_dev = slots // (count_fc * count_tok)
    slots_exp = slot_dev // w_in.shape[0]
    taps = conv_weight.shape[0]
    reach = taps // 2
    at_fc, at_tok = lax.axis_index("fc"), lax.axis_index("tok")
    other = [(i, i ^ 1) for i in range(count_fc)]
    cells = tokens.reshape(rows * cols, width)
    norm_gain, slot_gain = norm_gain.reshape(1, width), slot_gain.reshape(1, width)
    ln_gain, layer_scale = ln_gain.reshape(1, width), layer_scale.reshape(1, width)

    def shift(value, axis, step):
        count = lax.axis_size(axis)
        return lax.ppermute(value, axis, [(i, (i + step) % count) for i in range(count)])

    other = [(i, i ^ 1) for i in range(count_fc)]
    tie = lax.optimization_barrier
    even = at_tok % 2 == 0
    last = (rows - reach) * cols

    def swap(start):
        pairs = [(i, i + 1) for i in range(start, count_tok - 1, 2)]
        return pairs + [(j, i) for i, j in pairs]

    half = width // 2
    place = jnp.where(even, 0, last).reshape(1)
    in_other = lax.ppermute(w_in, "fc", other)
    out_other = lax.ppermute(w_out, "fc", other)

    index = jnp.stack([at_fc // 2, at_tok]).astype(jnp.int32)
    keys, *numer = dispatch(index, cells, slot_keys, norm_gain, (count_z, count_tok, slot_dev))
    numer[1], in_other, out_other = tie((numer[1], in_other, out_other))
    parts = [numer[0]] + [shift(numer[k], "tok", k) for k in range(1, count_tok)]

    first_halo = edge_rows(last - place, cells, reach * cols, 0, width, parts[1])
    first_halo = lax.ppermute(first_halo, "tok", swap(0))
    around = edge_rows(place, cells, reach * cols, half, half, parts[1])
    around = lax.ppermute(around, "tok", [(1, 3), (2, 0)] if count_tok == 4 else swap(1))

    slot_in = gather_slots(parts, slot_gain, count_z)
    arrived = [slot_in[0]] + [shift(slot_in[k], "fc", 2 * k) for k in range(1, count_z)]
    around, seen = after(around, slot_in[0]), slot_in[0]
    if count_tok == 4:
        around = lax.ppermute(around, "tok", [(3, 2), (0, 1)])
    always = jnp.ones((1,), jnp.int32)
    (share,) = combine_weights(always, [[cells]], keys, norm_gain, seen)
    core = (at_fc % 2).astype(jnp.int32).reshape(1)
    made = experts(core, share, arrived, w_in, w_out, in_other, out_other, slots_exp)
    direct = edge_rows(place, cells, reach * cols, 0, half, made[0])
    direct = lax.ppermute(direct, "tok", swap(1))
    back = [made[0]] + [shift(made[k], "fc", -2 * k) for k in range(1, count_z)]
    mine = jnp.concatenate(back, axis=0)
    above, below = at_tok > 0, at_tok < count_tok - 1
    inside = jnp.stack([jnp.where(even, below, above), jnp.where(even, above, below)])
    halo = ((first_halo,), (direct, around))
    freq, to_cols, fine, coef = wave(cols, taps)
    *halo_shares, filters = combine_weights(
        inside.astype(jnp.int32), halo, keys, norm_gain, made[0], (coef, conv_weight)
    )
    places = jnp.where(even, jnp.array([rows + reach, 0]), jnp.array([0, rows + reach]))
    every = [mine] + [shift(mine, "tok", -k) for k in range(1, count_tok)]

    fields = block_fields(
        (rows, cols, taps), places.astype(jnp.int32), cells, (first_halo, direct, around), (share, *halo_shares), filters,
        ln_gain, proj, layer_scale, every, (freq, to_cols, fine),
    )
    return fields.reshape(1, rows, cols, width)


def solution(mesh):
    return jax.shard_map(
        local,
        mesh=mesh,
        in_specs=(
            P("fc", "tok", None, None),
            P(),
            P(),
            P(),
            P(("fc", "tok"), None, None),
            P(("fc", "tok"), None, None),
            P(),
            P(),
            P(),
            P(),
        ),
        out_specs=P("fc", "tok", None, None),
        check_vma=False,
    )
```

```python
import functools

import jax
import jax.numpy as jnp
import ml_dtypes
import numpy as np
from jax import lax
from jax.experimental import pallas as pl
from jax.experimental.pallas import tpu as pltpu
from jax.sharding import PartitionSpec as P

F32 = jnp.float32
BF16 = jnp.bfloat16
LANES = 128
EPS = 1e-06
MIB = 1024 * 1024
LIMIT_D = 56
LIMIT_E = 16
NT = (((1,), (1,)), ((), ()))
VMEM = pl.BlockSpec(memory_space=pltpu.VMEM)
SMEM = pl.BlockSpec(memory_space=pltpu.SMEM)
HBM = pl.BlockSpec(memory_space=pltpu.HBM)
ANY = pl.BlockSpec(memory_space=pl.ANY)


def dot_nt(left, right):
    return lax.dot_general(left, right, NT, preferred_element_type=F32)


def rms_scale(value, gain):
    return value * lax.rsqrt(jnp.mean(value * value, axis=-1, keepdims=True) + EPS) * gain


def split_index(value, count):
    if count & (count - 1) == 0:
        return value >> (count.bit_length() - 1), value & (count - 1)
    return value // count, lax.rem(value, count)


def cost(flops, moved, exps=0):
    return pl.CostEstimate(flops=flops, bytes_accessed=moved, transcendentals=exps)


def dispatch_kernel(layout, index_ref, cells_hbm, keys_hbm, gain_ref, keys_out, *rest):
    count_z, count_tok, slot_dev = layout
    outs, (cells_ref, keys_ref, normed_ref, cell_sems, key_sem) = rest[:-5], rest[-5:]
    total, width = cells_ref.shape
    slots = keys_ref.shape[1]
    my_z, my_tok = index_ref[0], index_ref[1]
    count = cell_sems.shape[0]
    block = total // count
    key_copy = pltpu.make_async_copy(keys_hbm, keys_ref, key_sem)
    key_copy.start()
    copies = []
    for step in range(count):
        rows = slice(step * block, (step + 1) * block)
        copies.append(
            pltpu.make_async_copy(cells_hbm.at[rows], cells_ref.at[rows], cell_sems.at[step])
        )
        copies[-1].start()
    place = lax.broadcasted_iota(jnp.int32, (slots, 1), 0)
    source = lax.broadcasted_iota(jnp.int32, (slots, slots), 1)
    outer, inner = split_index(place, slot_dev)
    outer, core = split_index(outer, 2)
    step_tok, step_z = split_index(outer, count_z)
    at_z = split_index(step_z + my_z, count_z)[1]
    at_tok = split_index(step_tok + my_tok, count_tok)[1]
    wanted = ((at_z * 2 + core) * count_tok + at_tok) * slot_dev + inner
    pick = jnp.where(wanted == source, 1.0, 0.0).astype(BF16)
    key_copy.wait()
    keys = dot_nt(pick, keys_ref[...]).astype(BF16)
    keys_out[...] = keys

    for step in range(count):
        rows = slice(step * block, (step + 1) * block)
        copies[step].wait()
        normed_ref[rows, :] = rms_scale(cells_ref[rows, :].astype(F32), gain_ref[...]).astype(BF16)

    part = slots // count_tok
    logits = dot_nt(keys, normed_ref[...])
    peak = jnp.max(logits, axis=1, keepdims=True)
    weight = jnp.exp(logits - peak).astype(BF16)
    first = peak.astype(BF16).astype(F32)
    second = (peak - first).astype(BF16).astype(F32)
    third = peak - first - second
    lane = lax.broadcasted_iota(jnp.int32, (slots, LANES), 1)
    marks = jnp.where(
        lane == 0, first, jnp.where(lane == 1, second, jnp.where(lane == 2, third, 0.0))
    ).astype(BF16)
    for at, out in enumerate(outs):
        out[:, width:] = marks[at * part : (at + 1) * part, :]
    for lane in range(0, width, 2 * LANES):
        lanes = slice(lane, lane + 2 * LANES)
        numer = jnp.dot(weight, cells_ref[:, lanes], preferred_element_type=F32).astype(BF16)
        for at, out in enumerate(outs):
            out[:, lanes] = numer[at * part : (at + 1) * part, :]


def dispatch(index, cells, keys, gain, layout):
    count_z, count_tok, slot_dev = layout
    total, width = cells.shape
    slots = keys.shape[1]
    part = slots // count_tok
    count = 8
    return pl.pallas_call(
        functools.partial(dispatch_kernel, layout),
        out_shape=[jax.ShapeDtypeStruct((slots, width), BF16)]
        + [jax.ShapeDtypeStruct((part, width + LANES), BF16)] * count_tok,
        in_specs=[SMEM, HBM, HBM, VMEM],
        out_specs=[VMEM] * (1 + count_tok),
        scratch_shapes=[
            pltpu.VMEM((total, width), BF16),
            pltpu.VMEM((width, slots), BF16),
            pltpu.VMEM((total, width), BF16),
            pltpu.SemaphoreType.DMA((count,)),
            pltpu.SemaphoreType.DMA,
        ],
        compiler_params=pltpu.CompilerParams(vmem_limit_bytes=LIMIT_D * MIB),
        cost_estimate=cost(4 * total * width * slots, 4 * total * width, total * slots),
        name="dispatch",
    )(index, cells, keys, gain)


def gather_kernel(count_z, gain_ref, *refs):
    count = len(refs) - count_z
    parts, outs = refs[:count], refs[count:]
    width = gain_ref.shape[1]
    peaks = []
    for ref in parts:
        piece = ref[:, width:].astype(F32)
        peaks.append(jnp.sum(piece, axis=1, keepdims=True))
    peak = functools.reduce(jnp.maximum, peaks)
    numer = None
    for ref, own in zip(parts, peaks):
        term = ref[:, :width].astype(F32) * jnp.exp(own - peak)
        numer = term if numer is None else numer + term
    value = rms_scale(numer, gain_ref[...]).astype(BF16)
    rows = value.shape[0] // count_z
    for at, out in enumerate(outs):
        out[...] = value[at * rows : (at + 1) * rows, :]


def gather_slots(parts, gain, count_z):
    rows, width = parts[0].shape[0] // count_z, gain.shape[1]
    return pl.pallas_call(
        functools.partial(gather_kernel, count_z),
        out_shape=[jax.ShapeDtypeStruct((rows, width), BF16)] * count_z,
        in_specs=[VMEM] * (1 + len(parts)),
        out_specs=[VMEM] * count_z,
        compiler_params=pltpu.CompilerParams(vmem_limit_bytes=8 * MIB),
        cost_estimate=cost(8 * len(parts) * rows * count_z * width, 4 * rows * count_z * width),
        name="gather_slots",
    )(gain, *parts)


def expert_kernel(count_z, slots_exp, core_ref, _, in_own, out_own, in_other, out_other, *refs):
    parts, outs = refs[:count_z], refs[count_z : 2 * count_z]
    rows_ref, sum_ref, in_ref, out_ref, sems = refs[2 * count_z :]
    each = parts[0].shape[0]
    per_core = in_own.shape[0]
    copies = []
    for which, pair in enumerate(((in_own, out_own), (in_other, out_other))):
        for at in range(per_core):
            place = which * per_core + at
            for kind, (source, target) in enumerate(zip(pair, (in_ref, out_ref))):
                copies.append(
                    pltpu.make_async_copy(
                        source.at[at], target.at[place], sems.at[2 * place + kind]
                    )
                )
                copies[-1].start()
    for at, ref in enumerate(parts):
        rows_ref[at * each : (at + 1) * each, :] = ref[...]
    rows = rows_ref[...]
    place = lax.broadcasted_iota(jnp.int32, (rows.shape[0], 1), 0)
    expert = lax.rem(place, each) // slots_exp
    core = core_ref[0]

    for at in range(2 * per_core):
        held = core if at < per_core else 1 - core
        mine = expert == held * per_core + at % per_core
        copies[2 * at].wait()
        hidden = jax.nn.gelu(jnp.dot(rows, in_ref[at], preferred_element_type=F32))
        hidden = jnp.where(mine, hidden, 0.0).astype(BF16)
        copies[2 * at + 1].wait()
        made = jnp.dot(hidden, out_ref[at], preferred_element_type=F32)
        if at == 0:
            sum_ref[...] = made
        else:
            sum_ref[...] += made
    for at, out in enumerate(outs):
        out[...] = sum_ref[at * each : (at + 1) * each, :].astype(BF16)


def experts(core, after, parts, w_in, w_out, in_other, out_other, slots_exp):
    count_z = len(parts)
    each, width = parts[0].shape
    per_core, _, inner = w_in.shape
    rows = each * count_z
    return pl.pallas_call(
        functools.partial(expert_kernel, count_z, slots_exp),
        out_shape=[jax.ShapeDtypeStruct((each, width), BF16)] * count_z,
        in_specs=[SMEM, ANY, HBM, HBM, HBM, HBM] + [VMEM] * count_z,
        out_specs=[VMEM] * count_z,
        scratch_shapes=[
            pltpu.VMEM((rows, width), BF16),
            pltpu.VMEM((rows, width), F32),
            pltpu.VMEM((2 * per_core, width, inner), BF16),
            pltpu.VMEM((2 * per_core, inner, width), BF16),
            pltpu.SemaphoreType.DMA((4 * per_core,)),
        ],
        compiler_params=pltpu.CompilerParams(vmem_limit_bytes=LIMIT_E * MIB),
        cost_estimate=cost(8 * rows * width * inner * per_core, 8 * width * inner * per_core),
        name="experts",
    )(core, after, w_in, w_out, in_other, out_other, *parts)


def pass_kernel(value_ref, _, out_ref):
    out_ref[...] = value_ref[...]


def after(value, other):
    return pl.pallas_call(
        pass_kernel,
        out_shape=jax.ShapeDtypeStruct(value.shape, value.dtype),
        in_specs=[VMEM, ANY],
        out_specs=VMEM,
        compiler_params=pltpu.CompilerParams(vmem_limit_bytes=8 * MIB),
        cost_estimate=cost(0, 4 * value.size),
        name="after",
    )(value, other)


def copy_kernel(lane, start_ref, cells_ref, _, out_ref):
    rows, wide = out_ref.shape
    at = pl.ds(pl.multiple_of(start_ref[0], LANES), rows)
    out_ref[...] = cells_ref[at, lane : lane + wide]


def edge_rows(start, cells, rows, lane, wide, after):
    return pl.pallas_call(
        functools.partial(copy_kernel, lane),
        out_shape=jax.ShapeDtypeStruct((rows, wide), BF16),
        in_specs=[SMEM, VMEM, ANY],
        out_specs=VMEM,
        compiler_params=pltpu.CompilerParams(vmem_limit_bytes=8 * MIB),
        cost_estimate=cost(0, 4 * rows * cells.shape[1]),
        name="edge_rows",
    )(start, cells, after)


def combine_kernel(counts, valid_ref, keys_ref, gain_ref, _, *refs):
    block = 128
    total = sum(counts)
    sources, refs = refs[:total], refs[total:]
    if len(refs) > len(counts):
        fill_spectrum(refs[0], refs[1], refs[-1])
        refs = refs[2:-1]
    for at, (count, out_ref) in enumerate(zip(counts, refs)):
        held, sources = sources[:count], sources[count:]
        for start in range(0, out_ref.shape[0], block):
            rows = slice(start, start + block)
            cells = jnp.concatenate([ref[rows, :] for ref in held], axis=1).astype(F32)
            normed = rms_scale(cells, gain_ref[...]).astype(BF16)
            logits = dot_nt(normed, keys_ref[...])
            raised = jnp.exp(logits - jnp.max(logits, axis=-1, keepdims=True))
            share = raised * (1.0 / jnp.sum(raised, axis=-1, keepdims=True))
            out_ref[rows, :] = jnp.where(valid_ref[at] > 0, share, 0.0).astype(BF16)


def combine_weights(valid, cells, keys, gain, after, filters=()):
    made = [(filters[1].shape[0], filters[0].shape[0], filters[1].shape[2])] if filters else []
    width, slots = gain.shape[1], keys.shape[0]
    total = sum(parts[0].shape[0] for parts in cells)
    flat = [part for parts in cells for part in parts]
    return pl.pallas_call(
        functools.partial(combine_kernel, [len(parts) for parts in cells]),
        out_shape=[jax.ShapeDtypeStruct((parts[0].shape[0], slots), BF16) for parts in cells]
        + [jax.ShapeDtypeStruct(shape, F32) for shape in made],
        in_specs=[SMEM, VMEM, VMEM, ANY] + [VMEM] * (len(flat) + len(filters)),
        out_specs=[VMEM] * (len(cells) + len(made)),
        compiler_params=pltpu.CompilerParams(vmem_limit_bytes=16 * MIB),
        cost_estimate=cost(2 * total * width * slots, 2 * total * width, total * slots),
        name="combine_weights",
    )(valid, keys, gain, after, *flat, *filters)


def batch(rows):
    return next(count for count in (8, 4, 2, 1) if rows % count == 0)


def pieces(value, count):
    out = []
    for _ in range(count):
        piece = value.astype(BF16)
        out.append(piece)
        value = value - piece.astype(value.dtype)
    return out


def wave(cols, taps):
    half = cols // 2
    freq = np.arange(half)[:, None]
    angle = 2 * np.pi * ((freq * np.arange(cols)[None, :]) % cols) / cols
    sign = np.where(np.arange(cols) % 2 == 0, 1.0, -1.0)
    real, imag = np.cos(angle), -np.sin(angle)
    imag[0] = sign
    to_freq = np.concatenate([real, imag], axis=0)
    back_real, back_imag = 2 * np.cos(angle).T / cols, -2 * np.sin(angle).T / cols
    back_real[:, 0] = sign / cols
    back_imag[:, 0] = 1 / cols
    to_cols = np.concatenate([back_real, back_imag], axis=1)
    offset = np.arange(taps) - taps // 2
    turn = 2 * np.pi * freq * offset[None, :] / cols
    first, second, third = np.cos(turn), np.sin(turn) - np.cos(turn), np.sin(turn) + np.cos(turn)
    first[0], second[0] = 0.0, 1.0
    third[0] = np.where(offset % 2 == 0, -1.0, 1.0)
    spectrum = np.zeros((3 * half, 8))
    spectrum[:, :taps] = np.concatenate([first, second, third], axis=0)

    def split(value):
        high = value.astype(np.float32).astype(ml_dtypes.bfloat16)
        return high, (value - high.astype(np.float64)).astype(np.float32).astype(ml_dtypes.bfloat16)

    f_high, f_low = split(to_freq)
    c_high, c_low = split(to_cols)
    s_high, s_low = split(spectrum)
    return (
        np.concatenate([f_high, f_low], axis=1),
        np.concatenate([c_high, c_high], axis=1),
        c_low,
        np.concatenate([s_high, s_high, s_high, s_low, s_low], axis=1),
    )


def fill_spectrum(coef_ref, weight_ref, out_ref):
    taps, _, width = weight_ref.shape
    fill = jnp.zeros((8 - taps, width), F32)
    for tap in range(taps):
        row = jnp.concatenate([weight_ref[tap], fill], axis=0)
        one, two, three = (p.astype(F32) for p in pieces(row, 3))
        stack = jnp.concatenate([one, two, three, one, two], axis=0).astype(BF16)
        out_ref[tap] = jnp.dot(coef_ref[...], stack, preferred_element_type=F32)


def block_kernel(
    dims, place_ref, cells_ref, first_ref, second_a, second_b, share_ref, share_low, share_high, spectrum_ref, freq_ref,
    cols_ref, fine_ref, ln_ref, proj_ref, scale_ref, *rest
):
    rows, cols, taps = dims
    slot_refs, out_ref = rest[:-6], rest[-6]
    slots_ref, state_ref, freqs_ref, back_ref, conv_ref = rest[-5:]
    reach = taps // 2
    half = cols // 2
    width = cells_ref.shape[1]
    start = 0
    for ref in slot_refs:
        slots_ref[start : start + ref.shape[0], :] = ref[...]
        start += ref.shape[0]
    chunk = 2 * LANES

    def mix(cells, share, row, to, keep):
        at = pl.ds(pl.multiple_of(row * cols, cols), cols)
        picked = share[at, :]
        for lane in range(0, width, chunk):
            lanes = slice(lane, lane + chunk)
            mixed = jnp.dot(picked, slots_ref[:, lanes], preferred_element_type=F32)
            wide = cells[0].shape[1]
            held = cells[lane // wide][at, lane % wide : lane % wide + chunk]
            state = (held.astype(F32) + mixed).astype(BF16)
            if keep:
                state_ref[at, lanes] = state
            twice = jnp.concatenate([state, state], axis=0)
            freqs_ref[to, :, lanes] = jnp.dot(freq_ref[...], twice, preferred_element_type=F32)

    for row in range(reach):
        mix((first_ref,), share_low, row, row + place_ref[0], False)
        mix((second_a, second_b), share_high, row, row + place_ref[1], False)

    at_once = batch(rows)

    @pl.loop(0, rows // at_once)
    def _(step):
        for extra in range(at_once):
            row = step * at_once + extra
            mix((cells_ref,), share_ref, row, row + reach, True)

    tile = 16

    @pl.loop(0, width // LANES)
    def _(group):
        lanes = pl.ds(pl.multiple_of(group * LANES, LANES), LANES)

        @pl.loop(0, half // tile)
        def _(step):
            base = pl.multiple_of(step * tile, tile)
            for first in range(0, rows, 8):
                parts = ([], [])
                for sub in range(0, tile, 8):
                    real_at, imag_at = pl.ds(base + sub, 8), pl.ds(base + half + sub, 8)
                    third_at = pl.ds(base + 2 * half + sub, 8)
                    weights = [
                        [spectrum_ref[tap, at, lanes] for tap in range(taps)]
                        for at in (real_at, imag_at, third_at)
                    ]
                    sums = [[None] * 8 for _ in range(3)]
                    for row in range(8 + taps - 1):
                        real = freqs_ref[first + row, real_at, lanes]
                        imag = freqs_ref[first + row, imag_at, lanes]
                        for kind, value in enumerate((real + imag, real, imag)):
                            for to in range(max(0, row - taps + 1), min(8, row + 1)):
                                term = value * weights[kind][row - to]
                                have = sums[kind][to]
                                sums[kind][to] = term if have is None else have + term
                    parts[0].append([sums[0][to] - sums[2][to] for to in range(8)])
                    parts[1].append([sums[0][to] + sums[1][to] for to in range(8)])
                for to in range(8):
                    for which in range(2):
                        value = jnp.concatenate([sub[to] for sub in parts[which]], axis=0)
                        high, low = pieces(value, 2)
                        back_ref[first + to, pl.ds(base + which * half, tile), lanes] = high
                        back_ref[first + to, pl.ds(base + cols + which * half, tile), lanes] = low

    pair = batch(rows)

    @pl.loop(0, rows // pair)
    def _(step):
        for one in range(pair):
            total = None
            for lane in range(0, width, chunk):
                lanes = slice(lane, lane + chunk)
                row = step * pair + one
                conv = jnp.dot(cols_ref[...], back_ref[row, :, lanes], preferred_element_type=F32)
                conv += jnp.dot(fine_ref[...], back_ref[row, :cols, lanes], preferred_element_type=F32)
                conv_ref[one * cols : (one + 1) * cols, lanes] = conv
        at = pl.ds(pl.multiple_of(step * (pair * cols), pair * cols), pair * cols)
        conv = conv_ref[...]
        center = conv - jnp.mean(conv, axis=-1, keepdims=True)
        spread = jnp.mean(center * center, axis=-1, keepdims=True)
        normal = (center * lax.rsqrt(spread + EPS) * ln_ref[...]).astype(BF16)
        for lane in range(0, width, chunk):
            lanes = slice(lane, lane + chunk)
            branch = jnp.dot(normal, proj_ref[:, lanes], preferred_element_type=F32)
            branch = scale_ref[:, lanes] * jax.nn.gelu(branch)
            out_ref[at, lanes] = (state_ref[at, lanes].astype(F32) + branch).astype(BF16)


def block_fields(dims, places, cells, halo, shares, weight, ln_gain, proj, scale, slot_parts, waves):
    rows, cols, taps = dims
    total, width = cells.shape
    slots = sum(part.shape[0] for part in slot_parts)
    padded = rows + taps - 1
    return pl.pallas_call(
        functools.partial(block_kernel, dims),
        out_shape=jax.ShapeDtypeStruct((total, width), BF16),
        in_specs=[SMEM] + [VMEM] * (14 + len(slot_parts)),
        out_specs=VMEM,
        scratch_shapes=[
            pltpu.VMEM((slots, width), BF16),
            pltpu.VMEM((total, width), BF16),
            pltpu.VMEM((padded, cols, width), F32),
            pltpu.VMEM((rows, 2 * cols, width), BF16),
            pltpu.VMEM((batch(rows) * cols, width), F32),
        ],
        compiler_params=pltpu.CompilerParams(vmem_limit_bytes=32 * MIB),
        cost_estimate=cost(6 * total * width * width, 8 * total * width, total * width),
        name="block_fields",
    )(places, cells, *halo, *shares, weight, *waves, ln_gain, proj, scale, *slot_parts)


def local(
    tokens, slot_keys, norm_gain, slot_gain, w_in, w_out, conv_weight, ln_gain, proj, layer_scale
):
    rows, cols, width = tokens.shape[1:]
    count_fc = lax.axis_size("fc")
    count_tok = lax.axis_size("tok")
    count_z = count_fc // 2
    slots = slot_keys.shape[1]
    slot_dev = slots // (count_fc * count_tok)
    slots_exp = slot_dev // w_in.shape[0]
    taps = conv_weight.shape[0]
    reach = taps // 2
    at_fc, at_tok = lax.axis_index("fc"), lax.axis_index("tok")
    other = [(i, i ^ 1) for i in range(count_fc)]
    cells = tokens.reshape(rows * cols, width)
    norm_gain, slot_gain = norm_gain.reshape(1, width), slot_gain.reshape(1, width)
    ln_gain, layer_scale = ln_gain.reshape(1, width), layer_scale.reshape(1, width)

    def shift(value, axis, step):
        count = lax.axis_size(axis)
        return lax.ppermute(value, axis, [(i, (i + step) % count) for i in range(count)])

    other = [(i, i ^ 1) for i in range(count_fc)]
    tie = lax.optimization_barrier
    even = at_tok % 2 == 0
    last = (rows - reach) * cols

    def swap(start):
        pairs = [(i, i + 1) for i in range(start, count_tok - 1, 2)]
        return pairs + [(j, i) for i, j in pairs]

    half = width // 2
    place = jnp.where(even, 0, last).reshape(1)
    in_other = lax.ppermute(w_in, "fc", other)
    out_other = lax.ppermute(w_out, "fc", other)

    index = jnp.stack([at_fc // 2, at_tok]).astype(jnp.int32)
    keys, *numer = dispatch(index, cells, slot_keys, norm_gain, (count_z, count_tok, slot_dev))
    numer[1], in_other, out_other = tie((numer[1], in_other, out_other))
    parts = [numer[0]] + [shift(numer[k], "tok", k) for k in range(1, count_tok)]

    first_halo = edge_rows(last - place, cells, reach * cols, 0, width, parts[1])
    first_halo = lax.ppermute(first_halo, "tok", swap(0))
    around = edge_rows(place, cells, reach * cols, half, half, parts[1])
    around = lax.ppermute(around, "tok", [(1, 3), (2, 0)] if count_tok == 4 else swap(1))

    slot_in = gather_slots(parts, slot_gain, count_z)
    arrived = [slot_in[0]] + [shift(slot_in[k], "fc", 2 * k) for k in range(1, count_z)]
    around, seen = after(around, slot_in[0]), slot_in[0]
    if count_tok == 4:
        around = lax.ppermute(around, "tok", [(3, 2), (0, 1)])
    always = jnp.ones((1,), jnp.int32)
    (share,) = combine_weights(always, [[cells]], keys, norm_gain, seen)
    direct = edge_rows(place, cells, reach * cols, 0, half, share)
    direct = lax.ppermute(direct, "tok", swap(1))
    core = (at_fc % 2).astype(jnp.int32).reshape(1)
    made = experts(core, share, arrived, w_in, w_out, in_other, out_other, slots_exp)
    back = [made[0]] + [shift(made[k], "fc", -2 * k) for k in range(1, count_z)]
    mine = jnp.concatenate(back, axis=0)
    above, below = at_tok > 0, at_tok < count_tok - 1
    inside = jnp.stack([jnp.where(even, below, above), jnp.where(even, above, below)])
    halo = ((first_halo,), (direct, around))
    freq, to_cols, fine, coef = wave(cols, taps)
    *halo_shares, filters = combine_weights(
        inside.astype(jnp.int32), halo, keys, norm_gain, made[0], (coef, conv_weight)
    )
    places = jnp.where(even, jnp.array([rows + reach, 0]), jnp.array([0, rows + reach]))
    every = [mine] + [shift(mine, "tok", -k) for k in range(1, count_tok)]

    fields = block_fields(
        (rows, cols, taps), places.astype(jnp.int32), cells, (first_halo, direct, around), (share, *halo_shares), filters,
        ln_gain, proj, layer_scale, every, (freq, to_cols, fine),
    )
    return fields.reshape(1, rows, cols, width)


def solution(mesh):
    return jax.shard_map(
        local,
        mesh=mesh,
        in_specs=(
            P("fc", "tok", None, None),
            P(),
            P(),
            P(),
            P(("fc", "tok"), None, None),
            P(("fc", "tok"), None, None),
            P(),
            P(),
            P(),
            P(),
        ),
        out_specs=P("fc", "tok", None, None),
        check_vma=False,
    )
```

```python
import functools

import jax
import jax.numpy as jnp
import ml_dtypes
import numpy as np
from jax import lax
from jax.experimental import pallas as pl
from jax.experimental.pallas import tpu as pltpu
from jax.sharding import PartitionSpec as P

F32 = jnp.float32
BF16 = jnp.bfloat16
LANES = 128
EPS = 1e-06
MIB = 1024 * 1024
LIMIT_D = 56
LIMIT_E = 16
NT = (((1,), (1,)), ((), ()))
VMEM = pl.BlockSpec(memory_space=pltpu.VMEM)
SMEM = pl.BlockSpec(memory_space=pltpu.SMEM)
HBM = pl.BlockSpec(memory_space=pltpu.HBM)
ANY = pl.BlockSpec(memory_space=pl.ANY)


def dot_nt(left, right):
    return lax.dot_general(left, right, NT, preferred_element_type=F32)


def rms_scale(value, gain):
    return value * lax.rsqrt(jnp.mean(value * value, axis=-1, keepdims=True) + EPS) * gain


def paired(count):
    return count & (count - 1) == 0


def split_index(value, count):
    if count & (count - 1) == 0:
        return value >> (count.bit_length() - 1), value & (count - 1)
    return value // count, lax.rem(value, count)


def cost(flops, moved, exps=0):
    return pl.CostEstimate(flops=flops, bytes_accessed=moved, transcendentals=exps)


def dispatch_kernel(layout, index_ref, cells_hbm, keys_hbm, gain_ref, keys_out, *rest):
    count_z, count_tok, slot_dev = layout
    outs, (cells_ref, keys_ref, normed_ref, cell_sems, key_sem) = rest[:-5], rest[-5:]
    total, width = cells_ref.shape
    slots = keys_ref.shape[1]
    my_z, my_tok = index_ref[0], index_ref[1]
    count = cell_sems.shape[0]
    block = total // count
    key_copy = pltpu.make_async_copy(keys_hbm, keys_ref, key_sem)
    key_copy.start()
    copies = []
    for step in range(count):
        rows = slice(step * block, (step + 1) * block)
        copies.append(
            pltpu.make_async_copy(cells_hbm.at[rows], cells_ref.at[rows], cell_sems.at[step])
        )
        copies[-1].start()
    place = lax.broadcasted_iota(jnp.int32, (slots, 1), 0)
    source = lax.broadcasted_iota(jnp.int32, (slots, slots), 1)
    outer, inner = split_index(place, slot_dev)
    outer, core = split_index(outer, 2)
    step_tok, step_z = split_index(outer, count_z)
    at_z = step_z ^ my_z if paired(count_z) else split_index(step_z + my_z, count_z)[1]
    at_tok = split_index(step_tok + my_tok, count_tok)[1]
    wanted = ((at_z * 2 + core) * count_tok + at_tok) * slot_dev + inner
    pick = jnp.where(wanted == source, 1.0, 0.0).astype(BF16)
    key_copy.wait()
    keys = dot_nt(pick, keys_ref[...]).astype(BF16)
    keys_out[...] = keys

    for step in range(count):
        rows = slice(step * block, (step + 1) * block)
        copies[step].wait()
        normed_ref[rows, :] = rms_scale(cells_ref[rows, :].astype(F32), gain_ref[...]).astype(BF16)

    part = slots // count_tok
    logits = dot_nt(keys, normed_ref[...])
    peak = jnp.max(logits, axis=1, keepdims=True)
    weight = jnp.exp(logits - peak).astype(BF16)
    first = peak.astype(BF16).astype(F32)
    second = (peak - first).astype(BF16).astype(F32)
    third = peak - first - second
    lane = lax.broadcasted_iota(jnp.int32, (slots, LANES), 1)
    marks = jnp.where(
        lane == 0, first, jnp.where(lane == 1, second, jnp.where(lane == 2, third, 0.0))
    ).astype(BF16)
    for at, out in enumerate(outs):
        out[:, width:] = marks[at * part : (at + 1) * part, :]
    for lane in range(0, width, 2 * LANES):
        lanes = slice(lane, lane + 2 * LANES)
        numer = jnp.dot(weight, cells_ref[:, lanes], preferred_element_type=F32).astype(BF16)
        for at, out in enumerate(outs):
            out[:, lanes] = numer[at * part : (at + 1) * part, :]


def dispatch(index, cells, keys, gain, layout):
    count_z, count_tok, slot_dev = layout
    total, width = cells.shape
    slots = keys.shape[1]
    part = slots // count_tok
    count = 8
    return pl.pallas_call(
        functools.partial(dispatch_kernel, layout),
        out_shape=[jax.ShapeDtypeStruct((slots, width), BF16)]
        + [jax.ShapeDtypeStruct((part, width + LANES), BF16)] * count_tok,
        in_specs=[SMEM, HBM, HBM, VMEM],
        out_specs=[VMEM] * (1 + count_tok),
        scratch_shapes=[
            pltpu.VMEM((total, width), BF16),
            pltpu.VMEM((width, slots), BF16),
            pltpu.VMEM((total, width), BF16),
            pltpu.SemaphoreType.DMA((count,)),
            pltpu.SemaphoreType.DMA,
        ],
        compiler_params=pltpu.CompilerParams(vmem_limit_bytes=LIMIT_D * MIB),
        cost_estimate=cost(4 * total * width * slots, 4 * total * width, total * slots),
        name="dispatch",
    )(index, cells, keys, gain)


def gather_kernel(count_z, gain_ref, *refs):
    count = len(refs) - count_z
    parts, outs = refs[:count], refs[count:]
    width = gain_ref.shape[1]
    peaks = []
    for ref in parts:
        piece = ref[:, width:].astype(F32)
        peaks.append(jnp.sum(piece, axis=1, keepdims=True))
    peak = functools.reduce(jnp.maximum, peaks)
    numer = None
    for ref, own in zip(parts, peaks):
        term = ref[:, :width].astype(F32) * jnp.exp(own - peak)
        numer = term if numer is None else numer + term
    value = rms_scale(numer, gain_ref[...]).astype(BF16)
    rows = value.shape[0] // count_z
    for at, out in enumerate(outs):
        out[...] = value[at * rows : (at + 1) * rows, :]


def gather_slots(parts, gain, count_z):
    rows, width = parts[0].shape[0] // count_z, gain.shape[1]
    return pl.pallas_call(
        functools.partial(gather_kernel, count_z),
        out_shape=[jax.ShapeDtypeStruct((rows, width), BF16)] * count_z,
        in_specs=[VMEM] * (1 + len(parts)),
        out_specs=[VMEM] * count_z,
        compiler_params=pltpu.CompilerParams(vmem_limit_bytes=8 * MIB),
        cost_estimate=cost(8 * len(parts) * rows * count_z * width, 4 * rows * count_z * width),
        name="gather_slots",
    )(gain, *parts)


def expert_kernel(count_z, slots_exp, core_ref, _, in_own, out_own, in_other, out_other, *refs):
    parts, outs = refs[:count_z], refs[count_z : 2 * count_z]
    rows_ref, sum_ref, in_ref, out_ref, sems = refs[2 * count_z :]
    each = parts[0].shape[0]
    per_core = in_own.shape[0]
    copies = []
    for which, pair in enumerate(((in_own, out_own), (in_other, out_other))):
        for at in range(per_core):
            place = which * per_core + at
            for kind, (source, target) in enumerate(zip(pair, (in_ref, out_ref))):
                copies.append(
                    pltpu.make_async_copy(
                        source.at[at], target.at[place], sems.at[2 * place + kind]
                    )
                )
                copies[-1].start()
    for at, ref in enumerate(parts):
        rows_ref[at * each : (at + 1) * each, :] = ref[...]
    rows = rows_ref[...]
    place = lax.broadcasted_iota(jnp.int32, (rows.shape[0], 1), 0)
    expert = lax.rem(place, each) // slots_exp
    core = core_ref[0]

    for at in range(2 * per_core):
        held = core if at < per_core else 1 - core
        mine = expert == held * per_core + at % per_core
        copies[2 * at].wait()
        hidden = jax.nn.gelu(jnp.dot(rows, in_ref[at], preferred_element_type=F32))
        hidden = jnp.where(mine, hidden, 0.0).astype(BF16)
        copies[2 * at + 1].wait()
        made = jnp.dot(hidden, out_ref[at], preferred_element_type=F32)
        if at == 0:
            sum_ref[...] = made
        else:
            sum_ref[...] += made
    for at, out in enumerate(outs):
        out[...] = sum_ref[at * each : (at + 1) * each, :].astype(BF16)


def experts(core, after, parts, w_in, w_out, in_other, out_other, slots_exp):
    count_z = len(parts)
    each, width = parts[0].shape
    per_core, _, inner = w_in.shape
    rows = each * count_z
    return pl.pallas_call(
        functools.partial(expert_kernel, count_z, slots_exp),
        out_shape=[jax.ShapeDtypeStruct((each, width), BF16)] * count_z,
        in_specs=[SMEM, ANY, HBM, HBM, HBM, HBM] + [VMEM] * count_z,
        out_specs=[VMEM] * count_z,
        scratch_shapes=[
            pltpu.VMEM((rows, width), BF16),
            pltpu.VMEM((rows, width), F32),
            pltpu.VMEM((2 * per_core, width, inner), BF16),
            pltpu.VMEM((2 * per_core, inner, width), BF16),
            pltpu.SemaphoreType.DMA((4 * per_core,)),
        ],
        compiler_params=pltpu.CompilerParams(vmem_limit_bytes=LIMIT_E * MIB),
        cost_estimate=cost(8 * rows * width * inner * per_core, 8 * width * inner * per_core),
        name="experts",
    )(core, after, w_in, w_out, in_other, out_other, *parts)


def pass_kernel(value_ref, _, out_ref):
    out_ref[...] = value_ref[...]


def after(value, other):
    return pl.pallas_call(
        pass_kernel,
        out_shape=jax.ShapeDtypeStruct(value.shape, value.dtype),
        in_specs=[VMEM, ANY],
        out_specs=VMEM,
        compiler_params=pltpu.CompilerParams(vmem_limit_bytes=8 * MIB),
        cost_estimate=cost(0, 4 * value.size),
        name="after",
    )(value, other)


def copy_kernel(lane, start_ref, cells_ref, _, out_ref):
    rows, wide = out_ref.shape
    at = pl.ds(pl.multiple_of(start_ref[0], LANES), rows)
    out_ref[...] = cells_ref[at, lane : lane + wide]


def edge_rows(start, cells, rows, lane, wide, after):
    return pl.pallas_call(
        functools.partial(copy_kernel, lane),
        out_shape=jax.ShapeDtypeStruct((rows, wide), BF16),
        in_specs=[SMEM, VMEM, ANY],
        out_specs=VMEM,
        compiler_params=pltpu.CompilerParams(vmem_limit_bytes=8 * MIB),
        cost_estimate=cost(0, 4 * rows * cells.shape[1]),
        name="edge_rows",
    )(start, cells, after)


def combine_kernel(counts, valid_ref, keys_ref, gain_ref, _, *refs):
    block = 128
    total = sum(counts)
    sources, refs = refs[:total], refs[total:]
    if len(refs) > len(counts):
        fill_spectrum(refs[0], refs[1], refs[-1])
        refs = refs[2:-1]
    for at, (count, out_ref) in enumerate(zip(counts, refs)):
        held, sources = sources[:count], sources[count:]
        for start in range(0, out_ref.shape[0], block):
            rows = slice(start, start + block)
            cells = jnp.concatenate([ref[rows, :] for ref in held], axis=1).astype(F32)
            normed = rms_scale(cells, gain_ref[...]).astype(BF16)
            logits = dot_nt(normed, keys_ref[...])
            raised = jnp.exp(logits - jnp.max(logits, axis=-1, keepdims=True))
            share = raised * (1.0 / jnp.sum(raised, axis=-1, keepdims=True))
            out_ref[rows, :] = jnp.where(valid_ref[at] > 0, share, 0.0).astype(BF16)


def combine_weights(valid, cells, keys, gain, after, filters=()):
    made = [(filters[1].shape[0], filters[0].shape[0], filters[1].shape[2])] if filters else []
    width, slots = gain.shape[1], keys.shape[0]
    total = sum(parts[0].shape[0] for parts in cells)
    flat = [part for parts in cells for part in parts]
    return pl.pallas_call(
        functools.partial(combine_kernel, [len(parts) for parts in cells]),
        out_shape=[jax.ShapeDtypeStruct((parts[0].shape[0], slots), BF16) for parts in cells]
        + [jax.ShapeDtypeStruct(shape, F32) for shape in made],
        in_specs=[SMEM, VMEM, VMEM, ANY] + [VMEM] * (len(flat) + len(filters)),
        out_specs=[VMEM] * (len(cells) + len(made)),
        compiler_params=pltpu.CompilerParams(vmem_limit_bytes=16 * MIB),
        cost_estimate=cost(2 * total * width * slots, 2 * total * width, total * slots),
        name="combine_weights",
    )(valid, keys, gain, after, *flat, *filters)


def batch(rows):
    return next(count for count in (8, 4, 2, 1) if rows % count == 0)


def pieces(value, count):
    out = []
    for _ in range(count):
        piece = value.astype(BF16)
        out.append(piece)
        value = value - piece.astype(value.dtype)
    return out


def wave(cols, taps):
    half = cols // 2
    freq = np.arange(half)[:, None]
    angle = 2 * np.pi * ((freq * np.arange(cols)[None, :]) % cols) / cols
    sign = np.where(np.arange(cols) % 2 == 0, 1.0, -1.0)
    real, imag = np.cos(angle), -np.sin(angle)
    imag[0] = sign
    to_freq = np.concatenate([real, imag], axis=0)
    back_real, back_imag = 2 * np.cos(angle).T / cols, -2 * np.sin(angle).T / cols
    back_real[:, 0] = sign / cols
    back_imag[:, 0] = 1 / cols
    to_cols = np.concatenate([back_real, back_imag], axis=1)
    offset = np.arange(taps) - taps // 2
    turn = 2 * np.pi * freq * offset[None, :] / cols
    first, second, third = np.cos(turn), np.sin(turn) - np.cos(turn), np.sin(turn) + np.cos(turn)
    first[0], second[0] = 0.0, 1.0
    third[0] = np.where(offset % 2 == 0, -1.0, 1.0)
    spectrum = np.zeros((3 * half, 8))
    spectrum[:, :taps] = np.concatenate([first, second, third], axis=0)

    def split(value):
        high = value.astype(np.float32).astype(ml_dtypes.bfloat16)
        return high, (value - high.astype(np.float64)).astype(np.float32).astype(ml_dtypes.bfloat16)

    f_high, f_low = split(to_freq)
    c_high, c_low = split(to_cols)
    s_high, s_low = split(spectrum)
    return (
        np.concatenate([f_high, f_low], axis=1),
        np.concatenate([c_high, c_high], axis=1),
        c_low,
        np.concatenate([s_high, s_high, s_high, s_low, s_low], axis=1),
    )


def fill_spectrum(coef_ref, weight_ref, out_ref):
    taps, _, width = weight_ref.shape
    fill = jnp.zeros((8 - taps, width), F32)
    for tap in range(taps):
        row = jnp.concatenate([weight_ref[tap], fill], axis=0)
        one, two, three = (p.astype(F32) for p in pieces(row, 3))
        stack = jnp.concatenate([one, two, three, one, two], axis=0).astype(BF16)
        out_ref[tap] = jnp.dot(coef_ref[...], stack, preferred_element_type=F32)


def block_kernel(
    dims, place_ref, cells_ref, first_ref, second_a, second_b, share_ref, share_low, share_high, spectrum_ref, freq_ref,
    cols_ref, fine_ref, ln_ref, proj_ref, scale_ref, *rest
):
    rows, cols, taps = dims
    slot_refs, out_ref = rest[:-6], rest[-6]
    slots_ref, state_ref, freqs_ref, back_ref, conv_ref = rest[-5:]
    reach = taps // 2
    half = cols // 2
    width = cells_ref.shape[1]
    start = 0
    for ref in slot_refs:
        slots_ref[start : start + ref.shape[0], :] = ref[...]
        start += ref.shape[0]
    chunk = 2 * LANES

    def mix(cells, share, row, to, keep):
        at = pl.ds(pl.multiple_of(row * cols, cols), cols)
        picked = share[at, :]
        for lane in range(0, width, chunk):
            lanes = slice(lane, lane + chunk)
            mixed = jnp.dot(picked, slots_ref[:, lanes], preferred_element_type=F32)
            wide = cells[0].shape[1]
            held = cells[lane // wide][at, lane % wide : lane % wide + chunk]
            state = (held.astype(F32) + mixed).astype(BF16)
            if keep:
                state_ref[at, lanes] = state
            twice = jnp.concatenate([state, state], axis=0)
            freqs_ref[to, :, lanes] = jnp.dot(freq_ref[...], twice, preferred_element_type=F32)

    for row in range(reach):
        mix((first_ref,), share_low, row, row + place_ref[0], False)
        mix((second_a, second_b), share_high, row, row + place_ref[1], False)

    at_once = batch(rows)

    @pl.loop(0, rows // at_once)
    def _(step):
        for extra in range(at_once):
            row = step * at_once + extra
            mix((cells_ref,), share_ref, row, row + reach, True)

    tile = 16

    @pl.loop(0, width // LANES)
    def _(group):
        lanes = pl.ds(pl.multiple_of(group * LANES, LANES), LANES)

        @pl.loop(0, half // tile)
        def _(step):
            base = pl.multiple_of(step * tile, tile)
            for first in range(0, rows, 8):
                parts = ([], [])
                for sub in range(0, tile, 8):
                    real_at, imag_at = pl.ds(base + sub, 8), pl.ds(base + half + sub, 8)
                    third_at = pl.ds(base + 2 * half + sub, 8)
                    weights = [
                        [spectrum_ref[tap, at, lanes] for tap in range(taps)]
                        for at in (real_at, imag_at, third_at)
                    ]
                    sums = [[None] * 8 for _ in range(3)]
                    for row in range(8 + taps - 1):
                        real = freqs_ref[first + row, real_at, lanes]
                        imag = freqs_ref[first + row, imag_at, lanes]
                        for kind, value in enumerate((real + imag, real, imag)):
                            for to in range(max(0, row - taps + 1), min(8, row + 1)):
                                term = value * weights[kind][row - to]
                                have = sums[kind][to]
                                sums[kind][to] = term if have is None else have + term
                    parts[0].append([sums[0][to] - sums[2][to] for to in range(8)])
                    parts[1].append([sums[0][to] + sums[1][to] for to in range(8)])
                for to in range(8):
                    for which in range(2):
                        value = jnp.concatenate([sub[to] for sub in parts[which]], axis=0)
                        high, low = pieces(value, 2)
                        back_ref[first + to, pl.ds(base + which * half, tile), lanes] = high
                        back_ref[first + to, pl.ds(base + cols + which * half, tile), lanes] = low

    pair = batch(rows)

    @pl.loop(0, rows // pair)
    def _(step):
        for one in range(pair):
            total = None
            for lane in range(0, width, chunk):
                lanes = slice(lane, lane + chunk)
                row = step * pair + one
                conv = jnp.dot(cols_ref[...], back_ref[row, :, lanes], preferred_element_type=F32)
                conv += jnp.dot(fine_ref[...], back_ref[row, :cols, lanes], preferred_element_type=F32)
                conv_ref[one * cols : (one + 1) * cols, lanes] = conv
        at = pl.ds(pl.multiple_of(step * (pair * cols), pair * cols), pair * cols)
        conv = conv_ref[...]
        center = conv - jnp.mean(conv, axis=-1, keepdims=True)
        spread = jnp.mean(center * center, axis=-1, keepdims=True)
        normal = (center * lax.rsqrt(spread + EPS) * ln_ref[...]).astype(BF16)
        for lane in range(0, width, chunk):
            lanes = slice(lane, lane + chunk)
            branch = jnp.dot(normal, proj_ref[:, lanes], preferred_element_type=F32)
            branch = scale_ref[:, lanes] * jax.nn.gelu(branch)
            out_ref[at, lanes] = (state_ref[at, lanes].astype(F32) + branch).astype(BF16)


def block_fields(dims, places, cells, halo, shares, weight, ln_gain, proj, scale, slot_parts, waves):
    rows, cols, taps = dims
    total, width = cells.shape
    slots = sum(part.shape[0] for part in slot_parts)
    padded = rows + taps - 1
    return pl.pallas_call(
        functools.partial(block_kernel, dims),
        out_shape=jax.ShapeDtypeStruct((total, width), BF16),
        in_specs=[SMEM] + [VMEM] * (14 + len(slot_parts)),
        out_specs=VMEM,
        scratch_shapes=[
            pltpu.VMEM((slots, width), BF16),
            pltpu.VMEM((total, width), BF16),
            pltpu.VMEM((padded, cols, width), F32),
            pltpu.VMEM((rows, 2 * cols, width), BF16),
            pltpu.VMEM((batch(rows) * cols, width), F32),
        ],
        compiler_params=pltpu.CompilerParams(vmem_limit_bytes=32 * MIB),
        cost_estimate=cost(6 * total * width * width, 8 * total * width, total * width),
        name="block_fields",
    )(places, cells, *halo, *shares, weight, *waves, ln_gain, proj, scale, *slot_parts)


def local(
    tokens, slot_keys, norm_gain, slot_gain, w_in, w_out, conv_weight, ln_gain, proj, layer_scale
):
    rows, cols, width = tokens.shape[1:]
    count_fc = lax.axis_size("fc")
    count_tok = lax.axis_size("tok")
    count_z = count_fc // 2
    slots = slot_keys.shape[1]
    slot_dev = slots // (count_fc * count_tok)
    slots_exp = slot_dev // w_in.shape[0]
    taps = conv_weight.shape[0]
    reach = taps // 2
    at_fc, at_tok = lax.axis_index("fc"), lax.axis_index("tok")
    other = [(i, i ^ 1) for i in range(count_fc)]
    cells = tokens.reshape(rows * cols, width)
    norm_gain, slot_gain = norm_gain.reshape(1, width), slot_gain.reshape(1, width)
    ln_gain, layer_scale = ln_gain.reshape(1, width), layer_scale.reshape(1, width)

    def shift(value, axis, step):
        count = lax.axis_size(axis)
        return lax.ppermute(value, axis, [(i, (i + step) % count) for i in range(count)])

    def shift_z(value, step):
        if not paired(count_z):
            return shift(value, "fc", 2 * step)
        return lax.ppermute(value, "fc", [(i, i ^ (2 * abs(step))) for i in range(count_fc)])

    other = [(i, i ^ 1) for i in range(count_fc)]
    tie = lax.optimization_barrier
    even = at_tok % 2 == 0
    last = (rows - reach) * cols

    def swap(start):
        pairs = [(i, i + 1) for i in range(start, count_tok - 1, 2)]
        return pairs + [(j, i) for i, j in pairs]

    half = width // 2
    place = jnp.where(even, 0, last).reshape(1)
    in_other = lax.ppermute(w_in, "fc", other)
    out_other = lax.ppermute(w_out, "fc", other)

    index = jnp.stack([at_fc // 2, at_tok]).astype(jnp.int32)
    keys, *numer = dispatch(index, cells, slot_keys, norm_gain, (count_z, count_tok, slot_dev))
    numer[1], in_other, out_other = tie((numer[1], in_other, out_other))
    parts = [numer[0]] + [shift(numer[k], "tok", k) for k in range(1, count_tok)]

    first_halo = edge_rows(last - place, cells, reach * cols, 0, width, parts[1])
    first_halo = lax.ppermute(first_halo, "tok", swap(0))
    around = edge_rows(place, cells, reach * cols, half, half, parts[1])
    around = lax.ppermute(around, "tok", [(1, 3), (2, 0)] if count_tok == 4 else swap(1))

    slot_in = gather_slots(parts, slot_gain, count_z)
    arrived = [slot_in[0]] + [shift_z(slot_in[k], k) for k in range(1, count_z)]
    around, seen = after(around, slot_in[0]), slot_in[0]
    if count_tok == 4:
        around = lax.ppermute(around, "tok", [(3, 2), (0, 1)])
    always = jnp.ones((1,), jnp.int32)
    (share,) = combine_weights(always, [[cells]], keys, norm_gain, seen)
    direct = edge_rows(place, cells, reach * cols, 0, half, share)
    direct = lax.ppermute(direct, "tok", swap(1))
    core = (at_fc % 2).astype(jnp.int32).reshape(1)
    made = experts(core, share, arrived, w_in, w_out, in_other, out_other, slots_exp)
    back = [made[0]] + [shift_z(made[k], -k) for k in range(1, count_z)]
    mine = jnp.concatenate(back, axis=0)
    above, below = at_tok > 0, at_tok < count_tok - 1
    inside = jnp.stack([jnp.where(even, below, above), jnp.where(even, above, below)])
    halo = ((first_halo,), (direct, around))
    freq, to_cols, fine, coef = wave(cols, taps)
    *halo_shares, filters = combine_weights(
        inside.astype(jnp.int32), halo, keys, norm_gain, made[0], (coef, conv_weight)
    )
    places = jnp.where(even, jnp.array([rows + reach, 0]), jnp.array([0, rows + reach]))
    every = [mine] + [shift(mine, "tok", -k) for k in range(1, count_tok)]

    fields = block_fields(
        (rows, cols, taps), places.astype(jnp.int32), cells, (first_halo, direct, around), (share, *halo_shares), filters,
        ln_gain, proj, layer_scale, every, (freq, to_cols, fine),
    )
    return fields.reshape(1, rows, cols, width)


def solution(mesh):
    return jax.shard_map(
        local,
        mesh=mesh,
        in_specs=(
            P("fc", "tok", None, None),
            P(),
            P(),
            P(),
            P(("fc", "tok"), None, None),
            P(("fc", "tok"), None, None),
            P(),
            P(),
            P(),
            P(),
        ),
        out_specs=P("fc", "tok", None, None),
        check_vma=False,
    )
```

```python
import functools

import jax
import jax.numpy as jnp
import ml_dtypes
import numpy as np
from jax import lax
from jax.experimental import pallas as pl
from jax.experimental.pallas import tpu as pltpu
from jax.sharding import PartitionSpec as P

F32 = jnp.float32
BF16 = jnp.bfloat16
LANES = 128
EPS = 1e-06
MIB = 1024 * 1024
LIMIT_D = 56
LIMIT_E = 16
NT = (((1,), (1,)), ((), ()))
VMEM = pl.BlockSpec(memory_space=pltpu.VMEM)
SMEM = pl.BlockSpec(memory_space=pltpu.SMEM)
HBM = pl.BlockSpec(memory_space=pltpu.HBM)
ANY = pl.BlockSpec(memory_space=pl.ANY)


def dot_nt(left, right):
    return lax.dot_general(left, right, NT, preferred_element_type=F32)


def rms_scale(value, gain):
    return value * lax.rsqrt(jnp.mean(value * value, axis=-1, keepdims=True) + EPS) * gain


def paired(count):
    return count & (count - 1) == 0


def split_index(value, count):
    if count & (count - 1) == 0:
        return value >> (count.bit_length() - 1), value & (count - 1)
    return value // count, lax.rem(value, count)


def cost(flops, moved, exps=0):
    return pl.CostEstimate(flops=flops, bytes_accessed=moved, transcendentals=exps)


def dispatch_kernel(layout, index_ref, cells_hbm, keys_hbm, gain_ref, keys_out, *rest):
    count_z, count_tok, slot_dev = layout
    outs, (cells_ref, keys_ref, normed_ref, cell_sems, key_sem) = rest[:-5], rest[-5:]
    total, width = cells_ref.shape
    slots = keys_ref.shape[1]
    my_z, my_tok = index_ref[0], index_ref[1]
    count = cell_sems.shape[0]
    block = total // count
    key_copy = pltpu.make_async_copy(keys_hbm, keys_ref, key_sem)
    key_copy.start()
    copies = []
    for step in range(count):
        rows = slice(step * block, (step + 1) * block)
        copies.append(
            pltpu.make_async_copy(cells_hbm.at[rows], cells_ref.at[rows], cell_sems.at[step])
        )
        copies[-1].start()
    place = lax.broadcasted_iota(jnp.int32, (slots, 1), 0)
    source = lax.broadcasted_iota(jnp.int32, (slots, slots), 1)
    outer, inner = split_index(place, slot_dev)
    outer, core = split_index(outer, 2)
    step_tok, step_z = split_index(outer, count_z)
    at_z = step_z ^ my_z if paired(count_z) else split_index(step_z + my_z, count_z)[1]
    at_tok = split_index(step_tok + my_tok, count_tok)[1]
    wanted = ((at_z * 2 + core) * count_tok + at_tok) * slot_dev + inner
    pick = jnp.where(wanted == source, 1.0, 0.0).astype(BF16)
    key_copy.wait()
    keys = dot_nt(pick, keys_ref[...]).astype(BF16)
    keys_out[...] = keys

    for step in range(count):
        rows = slice(step * block, (step + 1) * block)
        copies[step].wait()
        normed_ref[rows, :] = rms_scale(cells_ref[rows, :].astype(F32), gain_ref[...]).astype(BF16)

    part = slots // count_tok
    logits = dot_nt(keys, normed_ref[...])
    peak = jnp.max(logits, axis=1, keepdims=True)
    weight = jnp.exp(logits - peak).astype(BF16)
    first = peak.astype(BF16).astype(F32)
    second = (peak - first).astype(BF16).astype(F32)
    third = peak - first - second
    lane = lax.broadcasted_iota(jnp.int32, (slots, LANES), 1)
    marks = jnp.where(
        lane == 0, first, jnp.where(lane == 1, second, jnp.where(lane == 2, third, 0.0))
    ).astype(BF16)
    for at, out in enumerate(outs):
        out[:, width:] = marks[at * part : (at + 1) * part, :]
    for lane in range(0, width, 2 * LANES):
        lanes = slice(lane, lane + 2 * LANES)
        numer = jnp.dot(weight, cells_ref[:, lanes], preferred_element_type=F32).astype(BF16)
        for at, out in enumerate(outs):
            out[:, lanes] = numer[at * part : (at + 1) * part, :]


def dispatch(index, cells, keys, gain, layout):
    count_z, count_tok, slot_dev = layout
    total, width = cells.shape
    slots = keys.shape[1]
    part = slots // count_tok
    count = 4
    return pl.pallas_call(
        functools.partial(dispatch_kernel, layout),
        out_shape=[jax.ShapeDtypeStruct((slots, width), BF16)]
        + [jax.ShapeDtypeStruct((part, width + LANES), BF16)] * count_tok,
        in_specs=[SMEM, HBM, HBM, VMEM],
        out_specs=[VMEM] * (1 + count_tok),
        scratch_shapes=[
            pltpu.VMEM((total, width), BF16),
            pltpu.VMEM((width, slots), BF16),
            pltpu.VMEM((total, width), BF16),
            pltpu.SemaphoreType.DMA((count,)),
            pltpu.SemaphoreType.DMA,
        ],
        compiler_params=pltpu.CompilerParams(vmem_limit_bytes=LIMIT_D * MIB),
        cost_estimate=cost(4 * total * width * slots, 4 * total * width, total * slots),
        name="dispatch",
    )(index, cells, keys, gain)


def gather_kernel(count_z, gain_ref, *refs):
    count = len(refs) - count_z
    parts, outs = refs[:count], refs[count:]
    width = gain_ref.shape[1]
    peaks = []
    for ref in parts:
        piece = ref[:, width:].astype(F32)
        peaks.append(jnp.sum(piece, axis=1, keepdims=True))
    peak = functools.reduce(jnp.maximum, peaks)
    numer = None
    for ref, own in zip(parts, peaks):
        term = ref[:, :width].astype(F32) * jnp.exp(own - peak)
        numer = term if numer is None else numer + term
    value = rms_scale(numer, gain_ref[...]).astype(BF16)
    rows = value.shape[0] // count_z
    for at, out in enumerate(outs):
        out[...] = value[at * rows : (at + 1) * rows, :]


def gather_slots(parts, gain, count_z):
    rows, width = parts[0].shape[0] // count_z, gain.shape[1]
    return pl.pallas_call(
        functools.partial(gather_kernel, count_z),
        out_shape=[jax.ShapeDtypeStruct((rows, width), BF16)] * count_z,
        in_specs=[VMEM] * (1 + len(parts)),
        out_specs=[VMEM] * count_z,
        compiler_params=pltpu.CompilerParams(vmem_limit_bytes=8 * MIB),
        cost_estimate=cost(8 * len(parts) * rows * count_z * width, 4 * rows * count_z * width),
        name="gather_slots",
    )(gain, *parts)


def expert_kernel(count_z, slots_exp, core_ref, _, in_own, out_own, in_other, out_other, *refs):
    parts, outs = refs[:count_z], refs[count_z : 2 * count_z]
    rows_ref, sum_ref, in_ref, out_ref, sems = refs[2 * count_z :]
    each = parts[0].shape[0]
    per_core = in_own.shape[0]
    copies = []
    for which, pair in enumerate(((in_own, out_own), (in_other, out_other))):
        for at in range(per_core):
            place = which * per_core + at
            for kind, (source, target) in enumerate(zip(pair, (in_ref, out_ref))):
                copies.append(
                    pltpu.make_async_copy(
                        source.at[at], target.at[place], sems.at[2 * place + kind]
                    )
                )
                copies[-1].start()
    for at, ref in enumerate(parts):
        rows_ref[at * each : (at + 1) * each, :] = ref[...]
    rows = rows_ref[...]
    place = lax.broadcasted_iota(jnp.int32, (rows.shape[0], 1), 0)
    expert = lax.rem(place, each) // slots_exp
    core = core_ref[0]

    for at in range(2 * per_core):
        held = core if at < per_core else 1 - core
        mine = expert == held * per_core + at % per_core
        copies[2 * at].wait()
        hidden = jax.nn.gelu(jnp.dot(rows, in_ref[at], preferred_element_type=F32))
        hidden = jnp.where(mine, hidden, 0.0).astype(BF16)
        copies[2 * at + 1].wait()
        made = jnp.dot(hidden, out_ref[at], preferred_element_type=F32)
        if at == 0:
            sum_ref[...] = made
        else:
            sum_ref[...] += made
    for at, out in enumerate(outs):
        out[...] = sum_ref[at * each : (at + 1) * each, :].astype(BF16)


def experts(core, after, parts, w_in, w_out, in_other, out_other, slots_exp):
    count_z = len(parts)
    each, width = parts[0].shape
    per_core, _, inner = w_in.shape
    rows = each * count_z
    return pl.pallas_call(
        functools.partial(expert_kernel, count_z, slots_exp),
        out_shape=[jax.ShapeDtypeStruct((each, width), BF16)] * count_z,
        in_specs=[SMEM, ANY, HBM, HBM, HBM, HBM] + [VMEM] * count_z,
        out_specs=[VMEM] * count_z,
        scratch_shapes=[
            pltpu.VMEM((rows, width), BF16),
            pltpu.VMEM((rows, width), F32),
            pltpu.VMEM((2 * per_core, width, inner), BF16),
            pltpu.VMEM((2 * per_core, inner, width), BF16),
            pltpu.SemaphoreType.DMA((4 * per_core,)),
        ],
        compiler_params=pltpu.CompilerParams(vmem_limit_bytes=LIMIT_E * MIB),
        cost_estimate=cost(8 * rows * width * inner * per_core, 8 * width * inner * per_core),
        name="experts",
    )(core, after, w_in, w_out, in_other, out_other, *parts)


def pass_kernel(value_ref, _, out_ref):
    out_ref[...] = value_ref[...]


def after(value, other):
    return pl.pallas_call(
        pass_kernel,
        out_shape=jax.ShapeDtypeStruct(value.shape, value.dtype),
        in_specs=[VMEM, ANY],
        out_specs=VMEM,
        compiler_params=pltpu.CompilerParams(vmem_limit_bytes=8 * MIB),
        cost_estimate=cost(0, 4 * value.size),
        name="after",
    )(value, other)


def copy_kernel(lane, start_ref, cells_ref, _, out_ref):
    rows, wide = out_ref.shape
    at = pl.ds(pl.multiple_of(start_ref[0], LANES), rows)
    out_ref[...] = cells_ref[at, lane : lane + wide]


def edge_rows(start, cells, rows, lane, wide, after):
    return pl.pallas_call(
        functools.partial(copy_kernel, lane),
        out_shape=jax.ShapeDtypeStruct((rows, wide), BF16),
        in_specs=[SMEM, VMEM, ANY],
        out_specs=VMEM,
        compiler_params=pltpu.CompilerParams(vmem_limit_bytes=8 * MIB),
        cost_estimate=cost(0, 4 * rows * cells.shape[1]),
        name="edge_rows",
    )(start, cells, after)


def combine_kernel(counts, valid_ref, keys_ref, gain_ref, _, *refs):
    block = 128
    total = sum(counts)
    sources, refs = refs[:total], refs[total:]
    if len(refs) > len(counts):
        fill_spectrum(refs[0], refs[1], refs[-1])
        refs = refs[2:-1]
    for at, (count, out_ref) in enumerate(zip(counts, refs)):
        held, sources = sources[:count], sources[count:]
        for start in range(0, out_ref.shape[0], block):
            rows = slice(start, start + block)
            cells = jnp.concatenate([ref[rows, :] for ref in held], axis=1).astype(F32)
            normed = rms_scale(cells, gain_ref[...]).astype(BF16)
            logits = dot_nt(normed, keys_ref[...])
            raised = jnp.exp(logits - jnp.max(logits, axis=-1, keepdims=True))
            share = raised * (1.0 / jnp.sum(raised, axis=-1, keepdims=True))
            out_ref[rows, :] = jnp.where(valid_ref[at] > 0, share, 0.0).astype(BF16)


def combine_weights(valid, cells, keys, gain, after, filters=()):
    made = [(filters[1].shape[0], filters[0].shape[0], filters[1].shape[2])] if filters else []
    width, slots = gain.shape[1], keys.shape[0]
    total = sum(parts[0].shape[0] for parts in cells)
    flat = [part for parts in cells for part in parts]
    return pl.pallas_call(
        functools.partial(combine_kernel, [len(parts) for parts in cells]),
        out_shape=[jax.ShapeDtypeStruct((parts[0].shape[0], slots), BF16) for parts in cells]
        + [jax.ShapeDtypeStruct(shape, F32) for shape in made],
        in_specs=[SMEM, VMEM, VMEM, ANY] + [VMEM] * (len(flat) + len(filters)),
        out_specs=[VMEM] * (len(cells) + len(made)),
        compiler_params=pltpu.CompilerParams(vmem_limit_bytes=16 * MIB),
        cost_estimate=cost(2 * total * width * slots, 2 * total * width, total * slots),
        name="combine_weights",
    )(valid, keys, gain, after, *flat, *filters)


def batch(rows):
    return next(count for count in (8, 4, 2, 1) if rows % count == 0)


def pieces(value, count):
    out = []
    for _ in range(count):
        piece = value.astype(BF16)
        out.append(piece)
        value = value - piece.astype(value.dtype)
    return out


def wave(cols, taps):
    half = cols // 2
    freq = np.arange(half)[:, None]
    angle = 2 * np.pi * ((freq * np.arange(cols)[None, :]) % cols) / cols
    sign = np.where(np.arange(cols) % 2 == 0, 1.0, -1.0)
    real, imag = np.cos(angle), -np.sin(angle)
    imag[0] = sign
    to_freq = np.concatenate([real, imag], axis=0)
    back_real, back_imag = 2 * np.cos(angle).T / cols, -2 * np.sin(angle).T / cols
    back_real[:, 0] = sign / cols
    back_imag[:, 0] = 1 / cols
    to_cols = np.concatenate([back_real, back_imag], axis=1)
    offset = np.arange(taps) - taps // 2
    turn = 2 * np.pi * freq * offset[None, :] / cols
    first, second, third = np.cos(turn), np.sin(turn) - np.cos(turn), np.sin(turn) + np.cos(turn)
    first[0], second[0] = 0.0, 1.0
    third[0] = np.where(offset % 2 == 0, -1.0, 1.0)
    spectrum = np.zeros((3 * half, 8))
    spectrum[:, :taps] = np.concatenate([first, second, third], axis=0)

    def split(value):
        high = value.astype(np.float32).astype(ml_dtypes.bfloat16)
        return high, (value - high.astype(np.float64)).astype(np.float32).astype(ml_dtypes.bfloat16)

    f_high, f_low = split(to_freq)
    c_high, c_low = split(to_cols)
    s_high, s_low = split(spectrum)
    return (
        np.concatenate([f_high, f_low], axis=1),
        np.concatenate([c_high, c_high], axis=1),
        c_low,
        np.concatenate([s_high, s_high, s_high, s_low, s_low], axis=1),
    )


def fill_spectrum(coef_ref, weight_ref, out_ref):
    taps, _, width = weight_ref.shape
    fill = jnp.zeros((8 - taps, width), F32)
    for tap in range(taps):
        row = jnp.concatenate([weight_ref[tap], fill], axis=0)
        one, two, three = (p.astype(F32) for p in pieces(row, 3))
        stack = jnp.concatenate([one, two, three, one, two], axis=0).astype(BF16)
        out_ref[tap] = jnp.dot(coef_ref[...], stack, preferred_element_type=F32)


def block_kernel(
    dims, place_ref, cells_ref, first_ref, second_a, second_b, share_ref, share_low, share_high, spectrum_ref, freq_ref,
    cols_ref, fine_ref, ln_ref, proj_ref, scale_ref, *rest
):
    rows, cols, taps = dims
    slot_refs, out_ref = rest[:-6], rest[-6]
    slots_ref, state_ref, freqs_ref, back_ref, conv_ref = rest[-5:]
    reach = taps // 2
    half = cols // 2
    width = cells_ref.shape[1]
    start = 0
    for ref in slot_refs:
        slots_ref[start : start + ref.shape[0], :] = ref[...]
        start += ref.shape[0]
    chunk = 2 * LANES

    def mix(cells, share, row, to, keep):
        at = pl.ds(pl.multiple_of(row * cols, cols), cols)
        picked = share[at, :]
        for lane in range(0, width, chunk):
            lanes = slice(lane, lane + chunk)
            mixed = jnp.dot(picked, slots_ref[:, lanes], preferred_element_type=F32)
            wide = cells[0].shape[1]
            held = cells[lane // wide][at, lane % wide : lane % wide + chunk]
            state = (held.astype(F32) + mixed).astype(BF16)
            if keep:
                state_ref[at, lanes] = state
            twice = jnp.concatenate([state, state], axis=0)
            freqs_ref[to, :, lanes] = jnp.dot(freq_ref[...], twice, preferred_element_type=F32)

    for row in range(reach):
        mix((first_ref,), share_low, row, row + place_ref[0], False)
        mix((second_a, second_b), share_high, row, row + place_ref[1], False)

    at_once = batch(rows)

    @pl.loop(0, rows // at_once)
    def _(step):
        for extra in range(at_once):
            row = step * at_once + extra
            mix((cells_ref,), share_ref, row, row + reach, True)

    tile = 16

    @pl.loop(0, width // LANES)
    def _(group):
        lanes = pl.ds(pl.multiple_of(group * LANES, LANES), LANES)

        @pl.loop(0, half // tile)
        def _(step):
            base = pl.multiple_of(step * tile, tile)
            for first in range(0, rows, 8):
                parts = ([], [])
                for sub in range(0, tile, 8):
                    real_at, imag_at = pl.ds(base + sub, 8), pl.ds(base + half + sub, 8)
                    third_at = pl.ds(base + 2 * half + sub, 8)
                    weights = [
                        [spectrum_ref[tap, at, lanes] for tap in range(taps)]
                        for at in (real_at, imag_at, third_at)
                    ]
                    sums = [[None] * 8 for _ in range(3)]
                    for row in range(8 + taps - 1):
                        real = freqs_ref[first + row, real_at, lanes]
                        imag = freqs_ref[first + row, imag_at, lanes]
                        for kind, value in enumerate((real + imag, real, imag)):
                            for to in range(max(0, row - taps + 1), min(8, row + 1)):
                                term = value * weights[kind][row - to]
                                have = sums[kind][to]
                                sums[kind][to] = term if have is None else have + term
                    parts[0].append([sums[0][to] - sums[2][to] for to in range(8)])
                    parts[1].append([sums[0][to] + sums[1][to] for to in range(8)])
                for to in range(8):
                    for which in range(2):
                        value = jnp.concatenate([sub[to] for sub in parts[which]], axis=0)
                        high, low = pieces(value, 2)
                        back_ref[first + to, pl.ds(base + which * half, tile), lanes] = high
                        back_ref[first + to, pl.ds(base + cols + which * half, tile), lanes] = low

    pair = batch(rows)

    @pl.loop(0, rows // pair)
    def _(step):
        for one in range(pair):
            total = None
            for lane in range(0, width, chunk):
                lanes = slice(lane, lane + chunk)
                row = step * pair + one
                conv = jnp.dot(cols_ref[...], back_ref[row, :, lanes], preferred_element_type=F32)
                conv += jnp.dot(fine_ref[...], back_ref[row, :cols, lanes], preferred_element_type=F32)
                conv_ref[one * cols : (one + 1) * cols, lanes] = conv
        at = pl.ds(pl.multiple_of(step * (pair * cols), pair * cols), pair * cols)
        conv = conv_ref[...]
        center = conv - jnp.mean(conv, axis=-1, keepdims=True)
        spread = jnp.mean(center * center, axis=-1, keepdims=True)
        normal = (center * lax.rsqrt(spread + EPS) * ln_ref[...]).astype(BF16)
        for lane in range(0, width, chunk):
            lanes = slice(lane, lane + chunk)
            branch = jnp.dot(normal, proj_ref[:, lanes], preferred_element_type=F32)
            branch = scale_ref[:, lanes] * jax.nn.gelu(branch)
            out_ref[at, lanes] = (state_ref[at, lanes].astype(F32) + branch).astype(BF16)


def block_fields(dims, places, cells, halo, shares, weight, ln_gain, proj, scale, slot_parts, waves):
    rows, cols, taps = dims
    total, width = cells.shape
    slots = sum(part.shape[0] for part in slot_parts)
    padded = rows + taps - 1
    return pl.pallas_call(
        functools.partial(block_kernel, dims),
        out_shape=jax.ShapeDtypeStruct((total, width), BF16),
        in_specs=[SMEM] + [VMEM] * (14 + len(slot_parts)),
        out_specs=VMEM,
        scratch_shapes=[
            pltpu.VMEM((slots, width), BF16),
            pltpu.VMEM((total, width), BF16),
            pltpu.VMEM((padded, cols, width), F32),
            pltpu.VMEM((rows, 2 * cols, width), BF16),
            pltpu.VMEM((batch(rows) * cols, width), F32),
        ],
        compiler_params=pltpu.CompilerParams(vmem_limit_bytes=32 * MIB),
        cost_estimate=cost(6 * total * width * width, 8 * total * width, total * width),
        name="block_fields",
    )(places, cells, *halo, *shares, weight, *waves, ln_gain, proj, scale, *slot_parts)


def local(
    tokens, slot_keys, norm_gain, slot_gain, w_in, w_out, conv_weight, ln_gain, proj, layer_scale
):
    rows, cols, width = tokens.shape[1:]
    count_fc = lax.axis_size("fc")
    count_tok = lax.axis_size("tok")
    count_z = count_fc // 2
    slots = slot_keys.shape[1]
    slot_dev = slots // (count_fc * count_tok)
    slots_exp = slot_dev // w_in.shape[0]
    taps = conv_weight.shape[0]
    reach = taps // 2
    at_fc, at_tok = lax.axis_index("fc"), lax.axis_index("tok")
    other = [(i, i ^ 1) for i in range(count_fc)]
    cells = tokens.reshape(rows * cols, width)
    norm_gain, slot_gain = norm_gain.reshape(1, width), slot_gain.reshape(1, width)
    ln_gain, layer_scale = ln_gain.reshape(1, width), layer_scale.reshape(1, width)

    def shift(value, axis, step):
        count = lax.axis_size(axis)
        return lax.ppermute(value, axis, [(i, (i + step) % count) for i in range(count)])

    def shift_z(value, step):
        if not paired(count_z):
            return shift(value, "fc", 2 * step)
        return lax.ppermute(value, "fc", [(i, i ^ (2 * abs(step))) for i in range(count_fc)])

    other = [(i, i ^ 1) for i in range(count_fc)]
    tie = lax.optimization_barrier
    even = at_tok % 2 == 0
    last = (rows - reach) * cols

    def swap(start):
        pairs = [(i, i + 1) for i in range(start, count_tok - 1, 2)]
        return pairs + [(j, i) for i, j in pairs]

    half = width // 2
    place = jnp.where(even, 0, last).reshape(1)
    in_other = lax.ppermute(w_in, "fc", other)
    out_other = lax.ppermute(w_out, "fc", other)

    index = jnp.stack([at_fc // 2, at_tok]).astype(jnp.int32)
    keys, *numer = dispatch(index, cells, slot_keys, norm_gain, (count_z, count_tok, slot_dev))
    numer[1], in_other, out_other = tie((numer[1], in_other, out_other))
    parts = [numer[0]] + [shift(numer[k], "tok", k) for k in range(1, count_tok)]

    first_halo = edge_rows(last - place, cells, reach * cols, 0, width, parts[1])
    first_halo = lax.ppermute(first_halo, "tok", swap(0))
    around = edge_rows(place, cells, reach * cols, half, half, parts[1])
    around = lax.ppermute(around, "tok", [(1, 3), (2, 0)] if count_tok == 4 else swap(1))

    slot_in = gather_slots(parts, slot_gain, count_z)
    arrived = [slot_in[0]] + [shift_z(slot_in[k], k) for k in range(1, count_z)]
    around, seen = after(around, slot_in[0]), slot_in[0]
    if count_tok == 4:
        around = lax.ppermute(around, "tok", [(3, 2), (0, 1)])
    always = jnp.ones((1,), jnp.int32)
    (share,) = combine_weights(always, [[cells]], keys, norm_gain, seen)
    direct = edge_rows(place, cells, reach * cols, 0, half, share)
    direct = lax.ppermute(direct, "tok", swap(1))
    core = (at_fc % 2).astype(jnp.int32).reshape(1)
    made = experts(core, share, arrived, w_in, w_out, in_other, out_other, slots_exp)
    back = [made[0]] + [shift_z(made[k], -k) for k in range(1, count_z)]
    mine = jnp.concatenate(back, axis=0)
    above, below = at_tok > 0, at_tok < count_tok - 1
    inside = jnp.stack([jnp.where(even, below, above), jnp.where(even, above, below)])
    halo = ((first_halo,), (direct, around))
    freq, to_cols, fine, coef = wave(cols, taps)
    *halo_shares, filters = combine_weights(
        inside.astype(jnp.int32), halo, keys, norm_gain, made[0], (coef, conv_weight)
    )
    places = jnp.where(even, jnp.array([rows + reach, 0]), jnp.array([0, rows + reach]))
    every = [mine] + [shift(mine, "tok", -k) for k in range(1, count_tok)]

    fields = block_fields(
        (rows, cols, taps), places.astype(jnp.int32), cells, (first_halo, direct, around), (share, *halo_shares), filters,
        ln_gain, proj, layer_scale, every, (freq, to_cols, fine),
    )
    return fields.reshape(1, rows, cols, width)


def solution(mesh):
    return jax.shard_map(
        local,
        mesh=mesh,
        in_specs=(
            P("fc", "tok", None, None),
            P(),
            P(),
            P(),
            P(("fc", "tok"), None, None),
            P(("fc", "tok"), None, None),
            P(),
            P(),
            P(),
            P(),
        ),
        out_specs=P("fc", "tok", None, None),
        check_vma=False,
    )
```
